512 devices in a mesh: fsdp: 32 (over z, x_hi, core), tensor: 16 (over x_lo, y).
Axes of the slice: x: 4 (x_hi: 2, x_lo: 2; x = x_hi * 2 + x_lo), y: 8, z: 8, core: 2. Of those that a mesh axis runs over, the one named last changes fastest.
Arguments:
- tokens: bfloat16 [352, 8192], P('fsdp', 'tensor'), may hold values from -6 to 6
- cotangent: bfloat16 [352, 8192], P('fsdp', 'tensor'), may hold values from -3 to 3
- gate_weight: bfloat16 [8192, 14336], P('fsdp', 'tensor'), may hold values from -0.0625 to 0.0625
- up_weight: bfloat16 [8192, 14336], P('fsdp', 'tensor'), may hold values from -0.0625 to 0.0625
- down_weight: bfloat16 [14336, 8192], P('tensor', 'fsdp'), may hold values from -0.046875 to 0.046875
Outputs:
- grad_tokens: bfloat16 [352, 8192], P('fsdp', 'tensor')
- grad_gate: bfloat16 [8192, 14336], P('fsdp', 'tensor')
- grad_up: bfloat16 [8192, 14336], P('fsdp', 'tensor')
- grad_down: bfloat16 [14336, 8192], P('tensor', 'fsdp')
The draws below stay inside these ranges and needn't reach their ends.
All inputs are finite; a program needn't handle non-finite values.
Results may differ from the reference program's by a relative error of at most 0.0049.
Values may be sent and summed in bfloat16 or wider, within the bound.
No kernel may reach another device: no remote copies, remote signals or barrier semaphores. Data moves between devices by JAX's collectives and lax.ppermute only.
A program may use at most 64 MiB of HBM per device.

```python
import jax
import jax.numpy as jnp
from jax import lax

D = 8192
FF = 14336
TOKENS = 352


def shard_levels(stream_key, extent, cuts, smallest, high):
    loudness = 1.0
    for dim, parts in cuts:
        heights = jax.random.uniform(jax.random.fold_in(jax.random.fold_in(stream_key, 6), dim), (parts,), jnp.float32, smallest / len(cuts), high / len(cuts))
        loudness = loudness * jnp.repeat(jnp.exp(heights), extent[dim] // parts).reshape((-1,) + (1,) * (len(extent) - 1 - dim))
    return loudness


def normal_values(key, extent, deviation, limit, shards=(), dtype=jnp.bfloat16):
    drawn = jax.random.normal(key, extent, jnp.float32) * deviation
    if len(shards) > 0:
        drawn = shard_levels(key, extent, shards, -0.22, 0.18) * drawn
    return jnp.clip(drawn, min=-limit, max=limit).astype(dtype)


def setup_inputs(seed: int = 0) -> dict:
    streams_of = jax.random.split(jax.random.key(seed), 6)
    return {
        "tokens": normal_values(streams_of[0], (TOKENS, D), 1.0, 6.0, ((0, 32), (1, 16))),
        "cotangent": normal_values(streams_of[1], (TOKENS, D), 0.5, 3.0, ((0, 32), (1, 16))),
        "gate_weight": normal_values(streams_of[2], (D, FF), D ** -0.5, 0.0625, ((0, 32), (1, 16))),
        "up_weight": normal_values(streams_of[3], (D, FF), D ** -0.5, 0.0625, ((0, 32), (1, 16))),
        "down_weight": normal_values(streams_of[4], (FF, D), FF ** -0.5, 0.046875, ((0, 16), (1, 32))),
    }


def reference(tokens, cotangent, gate_weight, up_weight, down_weight):
    contract_cols = (((1,), (1,)), ((), ()))
    contract_rows = (((0,), (0,)), ((), ()))
    gate = jnp.dot(tokens, gate_weight, preferred_element_type=jnp.float32)
    up = jnp.dot(tokens, up_weight, preferred_element_type=jnp.float32)
    back = lax.dot_general(cotangent, down_weight, contract_cols, preferred_element_type=jnp.float32)
    logistic = jax.nn.sigmoid(gate)
    hidden = (gate * logistic * up).astype(jnp.bfloat16)
    grad_gate_act = (back * up * logistic * (1.0 + gate * (1.0 - logistic))).astype(jnp.bfloat16)
    grad_up_act = (back * gate * logistic).astype(jnp.bfloat16)
    grad_down = lax.dot_general(hidden, cotangent, contract_rows, preferred_element_type=jnp.float32).astype(jnp.bfloat16)
    grad_gate = lax.dot_general(tokens, grad_gate_act, contract_rows, preferred_element_type=jnp.float32).astype(jnp.bfloat16)
    grad_up = lax.dot_general(tokens, grad_up_act, contract_rows, preferred_element_type=jnp.float32).astype(jnp.bfloat16)
    grad_tokens = lax.dot_general(grad_gate_act, gate_weight, contract_cols, preferred_element_type=jnp.float32)
    grad_tokens = grad_tokens + lax.dot_general(grad_up_act, up_weight, contract_cols, preferred_element_type=jnp.float32)
    return grad_tokens.astype(jnp.bfloat16), grad_gate, grad_up, grad_down
```

```python
import functools

import jax
import jax.numpy as jnp
from jax import lax
from jax.experimental import pallas as pl
from jax.experimental.pallas import tpu as pltpu
from jax.sharding import Mesh
from jax.sharding import PartitionSpec as P

F32, BF16 = jnp.float32, jnp.bfloat16
ALL = ("z", "xh", "core", "xl", "y")
FSDP = ("z", "xh", "core")
TENSOR = ("xl", "y")
CHIPS = ("z", "xh")

ROWS, HALF = 11, 176
UP, ACROSS, PER = 11, 7, 5
VMEM = pl.BlockSpec(memory_space=pltpu.VMEM)
SMEM = pl.BlockSpec(memory_space=pltpu.SMEM)
PARAMS = pltpu.CompilerParams(vmem_limit_bytes=40 * 1024 * 1024)


def call(kernel, out_shape, inputs, scratch=(), specs=None, flops=0):
    moved = sum(x.size * x.dtype.itemsize for x in inputs)
    moved += sum(s.size * s.dtype.itemsize for s in jax.tree.leaves(out_shape))
    return pl.pallas_call(
        kernel,
        out_shape=out_shape,
        in_specs=specs or [VMEM] * len(inputs),
        out_specs=jax.tree.map(lambda _: VMEM, out_shape),
        scratch_shapes=list(scratch),
        compiler_params=PARAMS,
        cost_estimate=pl.CostEstimate(flops=flops, bytes_accessed=moved, transcendentals=0),
    )(*inputs)


def shape(*dims, dtype=BF16):
    return jax.ShapeDtypeStruct(dims, dtype)


def tile(ref_or_value, j):
    return ref_or_value[:, j * 128 : (j + 1) * 128]


def pack_kernel(core, tok, cot, out, wide):
    odd = core[0] == 1
    for base, ref in ((0, tok), (4, cot)):
        rows = ref[...].astype(F32)
        for j in range(4):
            piece = jnp.where(odd, tile(rows, (j + 2) % 4), tile(rows, j))
            wide[pl.ds(base + j, ROWS, stride=8), :] = piece
    out[...] = wide[...].astype(BF16)


def put_tiles(out, m, value):
    for i in range(UP):
        for j in range(ACROSS):
            dest, slot = divmod(i * ACROSS + j, PER)
            row = (m * PER + slot) * 16
            out[dest, row : row + 16, :] = value[i * 16 : (i + 1) * 16, j * 128 : (j + 1) * 128]


def get_tiles(ref, m, out, first):
    for i in range(UP):
        for j in range(ACROSS):
            source, slot = divmod(i * ACROSS + j, PER)
            row = (m * PER + slot) * 16
            out[first + i * 16 : first + (i + 1) * 16, j * 128 : (j + 1) * 128] = ref[source, row : row + 16, :]


def forward_kernel(
    rows, gate_own, gate_oth, up_own, up_oth, down_own, down_oth, parts, x_own, x_oth, wide
):
    for t in range(16):
        wide[t * 88 : (t + 1) * 88, :] = rows[t].astype(F32)
    for j, (ref, at) in enumerate(
        ((x_own, 0), (x_own, 1), (x_oth, 0), (x_oth, 1), (x_own, 2), (x_own, 3), (x_oth, 2), (x_oth, 3))
    ):
        ref[:, at * 128 : (at + 1) * 128] = wide[pl.ds(j, HALF, stride=8), :].astype(BF16)
    by_cols = (((1,), (0,)), ((), ()))
    by_rows = (((1,), (1,)), ((), ()))
    for m, (own, oth, cols, dims) in enumerate(
        (
            (gate_own, gate_oth, slice(0, 256), by_cols),
            (up_own, up_oth, slice(0, 256), by_cols),
            (down_own, down_oth, slice(256, 512), by_rows),
        )
    ):
        total = lax.dot_general(x_own[:, cols], own[...], dims, preferred_element_type=F32)
        total = total + lax.dot_general(x_oth[:, cols], oth[...], dims, preferred_element_type=F32)
        put_tiles(parts, m, total.astype(BF16))
        parts[15, (m * PER + 2) * 16 : (m + 1) * PER * 16, :] = jnp.zeros((48, 128), BF16)


def activation_kernel(parts, grads, hiddens):
    size = PER * 16
    total = parts[0].astype(F32)
    for i in range(1, 16):
        total = total + parts[i].astype(F32)
    gate, up, back = total[:size], total[size : 2 * size], total[2 * size :]
    logistic = jax.nn.sigmoid(gate)
    hidden = (gate * logistic * up).astype(BF16)
    grad_gate_act = (back * up * logistic * (1.0 + gate * (1.0 - logistic))).astype(BF16)
    grad_up_act = (back * gate * logistic).astype(BF16)
    for i in range(16):
        grads[i, :size, :] = grad_gate_act
        grads[i, size:, :] = grad_up_act
        hiddens[i] = hidden


def token_grad_kernel(grads, gate_own, gate_oth, up_own, up_oth, out, gate_act, up_act, total, wide):
    get_tiles(grads, 0, gate_act, 0)
    get_tiles(grads, 1, up_act, 0)
    dims = (((1,), (1,)), ((), ()))
    for at, gate_weight, up_weight in ((0, gate_own, up_own), (256, gate_oth, up_oth)):
        part = lax.dot_general(gate_act[...], gate_weight[...], dims, preferred_element_type=F32)
        part = part + lax.dot_general(up_act[...], up_weight[...], dims, preferred_element_type=F32)
        total[:, at : at + 256] = part
    for t in range(16):
        for j in range(4):
            wide[j * ROWS : (j + 1) * ROWS, :] = total[t * ROWS : (t + 1) * ROWS, j * 128 : (j + 1) * 128]
        out[t] = wide[...].astype(BF16)


def token_sum_kernel(core, parts, out, total):
    odd = core[0] == 1
    acc = parts[0].astype(F32)
    for t in range(1, 16):
        acc = acc + parts[t].astype(F32)
    total[...] = acc
    for j in range(4):
        here = total[j * ROWS : (j + 1) * ROWS, :]
        there = total[(j + 2) % 4 * ROWS : ((j + 2) % 4 + 1) * ROWS, :]
        out[:, j * 128 : (j + 1) * 128] = jnp.where(odd, there, here).astype(BF16)


def weight_grad_kernel(
    x_own, x_got, grads, grads_got, hiddens, hiddens_got, grad_gate, grad_up, grad_down, x_all, act
):
    contract_rows = (((0,), (0,)), ((), ()))
    x_all[:HALF, :] = x_own[...]
    x_all[HALF:, :] = x_got[...]
    for m, (mine, got, out) in enumerate(((grads, grads_got, grad_gate), (grads, grads_got, grad_up))):
        get_tiles(mine, m, act, 0)
        get_tiles(got, m, act, HALF)
        out[...] = lax.dot_general(
            x_all[:, :256], act[...], contract_rows, preferred_element_type=F32
        ).astype(BF16)
    get_tiles(hiddens, 0, act, 0)
    get_tiles(hiddens_got, 0, act, HALF)
    grad_down[...] = lax.dot_general(
        act[...], x_all[:, 256:], contract_rows, preferred_element_type=F32
    ).astype(BF16)


def swap_cores(x):
    return lax.ppermute(x, "core", [(0, 1), (1, 0)])


def per_device(tokens, cotangent, gate_weight, up_weight, down_weight):
    core = jnp.reshape(lax.axis_index("core"), (1,)).astype(jnp.int32)
    there = [(f * 16 + t, (2 * t + f % 2) * 16 + f // 2) for f in range(32) for t in range(16)]
    home = [(b, a) for a, b in there]

    packed = call(
        pack_kernel,
        shape(88, 128),
        (core, tokens, cotangent),
        [pltpu.VMEM((88, 128), F32)],
        specs=[SMEM, VMEM, VMEM],
    )
    packed = lax.ppermute(packed, ALL, there)
    gate_oth, up_oth, down_oth = swap_cores(gate_weight), swap_cores(up_weight), swap_cores(down_weight)
    rows = lax.all_to_all(jnp.broadcast_to(packed[None], (16, 88, 128)), TENSOR, 0, 0, tiled=True)

    parts, x_own, x_oth = call(
        forward_kernel,
        (shape(16, 3 * PER * 16, 128), shape(HALF, 512), shape(HALF, 512)),
        (rows, gate_weight, gate_oth, up_weight, up_oth, down_weight, down_oth),
        [pltpu.VMEM((16 * 88, 128), F32)],
        flops=6 * HALF * 512 * 896,
    )
    parts = lax.all_to_all(parts, CHIPS, 0, 0, tiled=True)
    x_got = swap_cores(x_oth)

    grads, hiddens = call(
        activation_kernel,
        (shape(16, 2 * PER * 16, 128), shape(16, PER * 16, 128)),
        (parts,),
    )
    grads = lax.all_to_all(grads, CHIPS, 0, 0, tiled=True)
    hiddens = lax.all_to_all(hiddens, CHIPS, 0, 0, tiled=True)

    token_parts = call(
        token_grad_kernel,
        shape(16, 4 * ROWS, 128),
        (grads, gate_weight, gate_oth, up_weight, up_oth),
        [
            pltpu.VMEM((HALF, 896), BF16),
            pltpu.VMEM((HALF, 896), BF16),
            pltpu.VMEM((HALF, 512), F32),
            pltpu.VMEM((4 * ROWS, 128), F32),
        ],
        flops=4 * HALF * 512 * 896,
    )
    token_parts = lax.all_to_all(token_parts, TENSOR, 0, 0, tiled=True)
    grads_got, hiddens_got = swap_cores(grads), swap_cores(hiddens)

    grad_tokens = call(
        token_sum_kernel,
        shape(ROWS, 512),
        (core, token_parts),
        [pltpu.VMEM((4 * ROWS, 128), F32)],
        specs=[SMEM, VMEM],
    )
    grad_tokens = lax.ppermute(grad_tokens, ALL, home)

    grad_gate, grad_up, grad_down = call(
        weight_grad_kernel,
        (shape(256, 896), shape(256, 896), shape(896, 256)),
        (x_own, x_got, grads, grads_got, hiddens, hiddens_got),
        [pltpu.VMEM((2 * HALF, 512), BF16), pltpu.VMEM((2 * HALF, 896), BF16)],
        flops=6 * 2 * HALF * 256 * 896,
    )
    return (grad_tokens, grad_gate, grad_up, grad_down)


def solution(mesh):
    chips = Mesh(mesh.devices.reshape(8, 2, 2, 2, 8), ALL)
    rows, cols = P(FSDP, TENSOR), P(TENSOR, FSDP)
    return jax.shard_map(
        per_device,
        mesh=chips,
        in_specs=(rows, rows, rows, rows, cols),
        out_specs=(rows, rows, rows, cols),
        check_vma=False,
    )
```

```python
import functools

import jax
import jax.numpy as jnp
from jax import lax
from jax.experimental import pallas as pl
from jax.experimental.pallas import tpu as pltpu
from jax.sharding import Mesh
from jax.sharding import PartitionSpec as P

F32, BF16 = jnp.float32, jnp.bfloat16
ALL = ("z", "xh", "core", "xl", "y")
FSDP = ("z", "xh", "core")
TENSOR = ("xl", "y")

ROWS, QUARTER, PADDED = 11, 88, 96
UP, ACROSS, PER = 5, 7, 5
SIZE = PER * 16
VMEM = pl.BlockSpec(memory_space=pltpu.VMEM)
ANY = pl.BlockSpec(memory_space=pl.ANY)
SMEM = pl.BlockSpec(memory_space=pltpu.SMEM)
PARAMS = pltpu.CompilerParams(vmem_limit_bytes=24 * 1024 * 1024)


def call(kernel, out_shape, inputs, scratch=(), specs=None, flops=0, deps=()):
    moved = sum(x.size * x.dtype.itemsize for x in inputs)
    moved += sum(s.size * s.dtype.itemsize for s in jax.tree.leaves(out_shape))
    n = len(inputs)

    def body(*refs):
        kernel(*refs[:n], *refs[n + len(deps) :])

    return pl.pallas_call(
        body,
        out_shape=out_shape,
        in_specs=(specs or [VMEM] * n) + [VMEM] * len(deps),
        out_specs=jax.tree.map(lambda _: VMEM, out_shape),
        scratch_shapes=list(scratch),
        compiler_params=PARAMS,
        cost_estimate=pl.CostEstimate(flops=flops, bytes_accessed=moved, transcendentals=0),
    )(*inputs, *deps)


def shape(*dims, dtype=BF16):
    return jax.ShapeDtypeStruct(dims, dtype)


def tile(ref_or_value, j):
    return ref_or_value[:, j * 128 : (j + 1) * 128]


def pack_kernel(core, tok, cot, out, wide):
    odd = core[0] == 1
    for base, ref in ((0, tok), (4, cot)):
        rows = ref[...].astype(F32)
        for j in range(4):
            piece = jnp.where(odd, tile(rows, (j + 2) % 4), tile(rows, j))
            wide[pl.ds(base + j, ROWS, stride=8), :] = piece
    out[...] = wide[...].astype(BF16)


def put_tiles(out, m, value):
    def put(slot, rows):
        row = m * SIZE + slot % PER * 16
        out[slot // PER, row : row + 16, :] = rows.astype(BF16)

    blank = jnp.zeros((8, 128), F32)
    for i in range(UP):
        for j in range(ACROSS):
            put(i * ACROSS + j, tile(value[i * 16 : (i + 1) * 16], j))
    last = [tile(value[UP * 16 : QUARTER], j) for j in range(ACROSS)] + [blank] * 3
    for j in range(0, 10, 2):
        put(UP * ACROSS + j // 2, jnp.concatenate([last[j], last[j + 1]], axis=0))


def get_tiles(ref, m, out, first):
    def get(slot):
        row = m * SIZE + slot % PER * 16
        return ref[slot // PER, row : row + 16, :]

    blank = jnp.zeros((8, 128), F32)
    for i in range(UP):
        for j in range(ACROSS):
            out[first + i * 16 : first + (i + 1) * 16, j * 128 : (j + 1) * 128] = get(i * ACROSS + j)
    for j in range(ACROSS):
        pair = get(UP * ACROSS + j // 2).astype(F32)
        half = pair[8:] if j % 2 else pair[:8]
        rows = jnp.concatenate([half, blank], axis=0).astype(BF16)
        out[first + UP * 16 : first + PADDED, j * 128 : (j + 1) * 128] = rows


def weights_kernel(gate_weight, up_weight, down_weight, out, down, sems):
    copies = [
        pltpu.make_async_copy(down_weight, down, sems.at[0]),
        pltpu.make_async_copy(gate_weight, out.at[:256], sems.at[1]),
        pltpu.make_async_copy(up_weight, out.at[256:512], sems.at[2]),
    ]
    for copy in copies:
        copy.start()
    for copy in copies:
        copy.wait()
    out[512:, :] = down[...].T


def spread_kernel(packed, out):
    for t in range(16):
        out[t] = packed[...]


def forward_kernel(rows, w0, w1, w2, w3, parts, x0, x1, x23, wide):
    for t in range(16):
        wide[t * 88 : (t + 1) * 88, :] = rows[t].astype(F32)
    blank = jnp.zeros((PADDED - QUARTER, 128), F32)
    for far in range(2):
        for j in range(8):
            piece = jnp.concatenate([wide[pl.ds(far * 704 + j, QUARTER, stride=8), :], blank], axis=0)
            at = (j // 4 * 2 + j % 2) * 128
            k = 2 * far + j % 4 // 2
            ref, first = ((x0, 0), (x1, 0), (x23, 0), (x23, PADDED))[k]
            ref[first : first + PADDED, at : at + 128] = piece.astype(BF16)
    blocks = (x0[...], x1[...], x23[:PADDED], x23[PADDED:])
    for m in range(3):
        cols = slice(256, 512) if m == 2 else slice(0, 256)
        total = jnp.zeros((PADDED, 896), F32)
        for x, w in zip(blocks, (w0, w1, w2, w3)):
            total = total + jnp.dot(x[:, cols], w[m * 256 : (m + 1) * 256, :], preferred_element_type=F32)
        put_tiles(parts, m, total)


def activation_kernel(parts, acts):
    total = parts[0].astype(F32)
    for i in range(1, 8):
        total = total + parts[i].astype(F32)
    gate, up, back = total[:SIZE], total[SIZE : 2 * SIZE], total[2 * SIZE :]
    logistic = jax.nn.sigmoid(gate)
    hidden = (gate * logistic * up).astype(BF16)
    grad_gate_act = (back * up * logistic * (1.0 + gate * (1.0 - logistic))).astype(BF16)
    grad_up_act = (back * gate * logistic).astype(BF16)
    for i in range(8):
        acts[i, :SIZE, :] = grad_gate_act
        acts[i, SIZE : 2 * SIZE, :] = grad_up_act
        acts[i, 2 * SIZE :, :] = hidden


def token_grad_kernel(acts, w0, w1, w2, w3, out, gate_act, up_act, total, wide):
    get_tiles(acts, 0, gate_act, 0)
    get_tiles(acts, 1, up_act, 0)
    dims = (((1,), (1,)), ((), ()))
    for k, w in enumerate((w0, w1, w2, w3)):
        part = lax.dot_general(gate_act[...], w[:256, :], dims, preferred_element_type=F32)
        part = part + lax.dot_general(up_act[...], w[256:512, :], dims, preferred_element_type=F32)
        total[:, k * 256 : (k + 1) * 256] = part
    for far in range(2):
        for i in range(8):
            for j in range(4):
                at = far * 512 + j * 128
                wide[j * ROWS : (j + 1) * ROWS, :] = total[i * ROWS : (i + 1) * ROWS, at : at + 128]
            out[far * 8 + i] = wide[...].astype(BF16)


def token_sum_kernel(core, parts, out, total):
    odd = core[0] == 1
    acc = parts[0].astype(F32)
    for t in range(1, 16):
        acc = acc + parts[t].astype(F32)
    total[...] = acc
    for j in range(4):
        here = total[j * ROWS : (j + 1) * ROWS, :]
        there = total[(j + 2) % 4 * ROWS : ((j + 2) % 4 + 1) * ROWS, :]
        out[:, j * 128 : (j + 1) * 128] = jnp.where(odd, there, here).astype(BF16)


def weight_grad_kernel(x0, x2, x13, acts0, acts1, acts2, acts3, grad_gate, grad_up, grad_down, x, act):
    contract_rows = (((0,), (0,)), ((), ()))
    x[:PADDED, :] = x0[...]
    x[PADDED : 2 * PADDED, :] = x13[:PADDED, :]
    x[2 * PADDED : 3 * PADDED, :] = x2[:PADDED, :]
    x[3 * PADDED :, :] = x13[PADDED:, :]
    for m in range(3):
        for k, acts in enumerate((acts0, acts1, acts2, acts3)):
            get_tiles(acts, m, act, k * PADDED)
        if m < 2:
            out, left, right = (grad_gate, grad_up)[m], x[:, :256], act[...]
        else:
            out, left, right = grad_down, act[...], x[:, 256:]
        out[...] = lax.dot_general(left, right, contract_rows, preferred_element_type=F32).astype(BF16)


def copy_kernel(x, out):
    out[...] = x[...]


def after(x, *deps):
    return call(copy_kernel, shape(*x.shape, dtype=x.dtype), (x,), deps=deps)


def swap(axis, x):
    return lax.ppermute(x, axis, [(0, 1), (1, 0)])


def place(z, xh, core, xl, y):
    return (((z * 2 + xh) * 2 + core) * 2 + xl) * 8 + y


def per_device(tokens, cotangent, gate_weight, up_weight, down_weight):
    core = jnp.reshape(lax.axis_index("core"), (1,)).astype(jnp.int32)
    there = [
        (place(z, xh, c, xl, y), place(4 * xl + y // 2, xh, c, y % 2 ^ xh, z))
        for z in range(8)
        for xh in range(2)
        for c in range(2)
        for xl in range(2)
        for y in range(8)
    ]
    home = [(b, a) for a, b in there]

    w0 = call(
        weights_kernel,
        shape(768, 896),
        (gate_weight, up_weight, down_weight),
        [pltpu.VMEM((896, 256), BF16), pltpu.SemaphoreType.DMA((3,))],
        specs=[ANY] * 3,
    )
    w2 = swap("xh", w0)
    packed = call(
        pack_kernel,
        shape(88, 128),
        (core, tokens, cotangent),
        [pltpu.VMEM((88, 128), F32)],
        specs=[SMEM, VMEM, VMEM],
    )
    packed = lax.ppermute(packed, ALL, there)
    w1 = swap("core", after(w0, packed))
    rows = lax.all_to_all(call(spread_kernel, shape(16, 88, 128), (packed,)), TENSOR, 0, 0, tiled=True)
    w2 = after(w2, rows)
    w3 = swap("core", w2)

    parts, x0, x1, x23 = call(
        forward_kernel,
        (shape(8, 3 * SIZE, 128), shape(PADDED, 512), shape(PADDED, 512), shape(2 * PADDED, 512)),
        (rows, w0, w1, w2, w3),
        [pltpu.VMEM((16 * 88, 128), F32)],
        flops=6 * PADDED * 1024 * 896,
    )
    parts = lax.all_to_all(parts, "z", 0, 0, tiled=True)
    x2 = swap("xh", after(x23, parts))
    x13 = swap("core", jnp.concatenate([x1, x2[PADDED:]], axis=0))

    acts0 = lax.all_to_all(call(activation_kernel, shape(8, 3 * SIZE, 128), (parts,)), "z", 0, 0, tiled=True)
    acts2 = swap("xh", acts0)

    token_parts = call(
        token_grad_kernel,
        shape(16, 4 * ROWS, 128),
        (acts0, w0, w1, w2, w3),
        [
            pltpu.VMEM((PADDED, 896), BF16),
            pltpu.VMEM((PADDED, 896), BF16),
            pltpu.VMEM((PADDED, 1024), F32),
            pltpu.VMEM((4 * ROWS, 128), F32),
        ],
        flops=4 * PADDED * 1024 * 896,
        deps=(x13,),
    )
    token_parts = lax.all_to_all(token_parts, TENSOR, 0, 0, tiled=True)
    acts0, acts2 = after(acts0, token_parts), after(acts2, token_parts)
    acts1, acts3 = swap("core", acts0), swap("core", acts2)

    grad_tokens = call(
        token_sum_kernel,
        shape(ROWS, 512),
        (core, token_parts),
        [pltpu.VMEM((4 * ROWS, 128), F32)],
        specs=[SMEM, VMEM],
    )
    grad_tokens = lax.ppermute(grad_tokens, ALL, home)

    grad_gate, grad_up, grad_down = call(
        weight_grad_kernel,
        (shape(256, 896), shape(256, 896), shape(896, 256)),
        (x0, x2, x13, acts0, acts1, acts2, acts3),
        [pltpu.VMEM((4 * PADDED, 512), BF16), pltpu.VMEM((4 * PADDED, 896), BF16)],
        flops=6 * 4 * PADDED * 256 * 896,
    )
    return (grad_tokens, grad_gate, grad_up, grad_down)


def solution(mesh):
    chips = Mesh(mesh.devices.reshape(8, 2, 2, 2, 8), ALL)
    rows, cols = P(FSDP, TENSOR), P(TENSOR, FSDP)
    return jax.shard_map(
        per_device,
        mesh=chips,
        in_specs=(rows, rows, rows, rows, cols),
        out_specs=(rows, rows, rows, cols),
        check_vma=False,
    )
```

```python
import math

import jax
import jax.numpy as jnp
from jax import lax
from jax.experimental import pallas as pl
from jax.experimental.pallas import tpu as pltpu
from jax.sharding import Mesh
from jax.sharding import PartitionSpec as P

F32, BF16 = jnp.float32, jnp.bfloat16
ALL = ("z", "xh", "core", "xl", "y")
FSDP = ("z", "xh", "core")
TENSOR = ("xl", "y")

ROWS, QUARTER, PADDED = 11, 88, 96
UP, ACROSS, PER = 5, 7, 5
SIZE = PER * 16
VMEM = pl.BlockSpec(memory_space=pltpu.VMEM)
HBM = pl.BlockSpec(memory_space=pltpu.HBM)
SMEM = pl.BlockSpec(memory_space=pltpu.SMEM)
PARAMS = pltpu.CompilerParams(vmem_limit_bytes=20 * 1024 * 1024)


def call(kernel, out_shape, inputs, scratch=(), specs=None, flops=0, deps=(), outs=None):
    moved = sum(x.size * x.dtype.itemsize for x in inputs)
    moved += sum(math.prod(s.shape) * s.dtype.itemsize for s in out_shape)
    n, m = len(inputs), len(out_shape)

    def body(*refs):
        rest = refs[n + len(deps) :]
        rest[m][...] = jnp.zeros((8, 128), F32)
        kernel(*refs[:n], *rest[:m], *rest[m + 1 :])

    return pl.pallas_call(
        body,
        out_shape=(*out_shape, shape(8, 128, dtype=F32)),
        in_specs=list(specs or [VMEM] * n) + [VMEM] * len(deps),
        out_specs=list(outs or [VMEM] * m) + [VMEM],
        scratch_shapes=list(scratch),
        compiler_params=PARAMS,
        cost_estimate=pl.CostEstimate(flops=flops, bytes_accessed=moved, transcendentals=0),
    )(*inputs, *deps)


def shape(*dims, dtype=BF16):
    return jax.ShapeDtypeStruct(dims, dtype)


def tile(ref_or_value, j):
    return ref_or_value[:, j * 128 : (j + 1) * 128]


def fetch(sems, *pairs):
    copies = [pltpu.make_async_copy(source, to, sems.at[i]) for i, (source, to) in enumerate(pairs)]
    for copy in copies:
        copy.start()
    for copy in copies:
        copy.wait()


def pack_kernel(place, tok, cot, out, wide):
    odd = place[0] == 1
    for base, ref in ((0, tok), (4, cot)):
        rows = ref[...].astype(F32)
        for j in range(4):
            piece = jnp.where(odd, tile(rows, (j + 2) % 4), tile(rows, j))
            wide[pl.ds(base + j, ROWS, stride=8), :] = piece
    out[...] = wide[...].astype(BF16)


def put_tiles(out, m, value, half):
    def put(slot, rows):
        row = m * SIZE + slot % PER * 16
        out[slot // PER * 2 + half, row : row + 16, :] = rows.astype(BF16)

    blank = jnp.zeros((8, 128), F32)
    for i in range(UP):
        for j in range(ACROSS):
            put(i * ACROSS + j, tile(value[i * 16 : (i + 1) * 16], j))
    last = [tile(value[UP * 16 : QUARTER], j) for j in range(ACROSS)] + [blank] * 3
    for j in range(0, 10, 2):
        put(UP * ACROSS + j // 2, jnp.concatenate([last[j], last[j + 1]], axis=0))


def get_tiles(ref, m, out, first):
    def get(slot):
        row = m * SIZE + slot % PER * 16
        return ref[slot // PER, row : row + 16, :]

    blank = jnp.zeros((8, 128), F32)
    for i in range(UP):
        for j in range(ACROSS):
            out[first + i * 16 : first + (i + 1) * 16, j * 128 : (j + 1) * 128] = get(i * ACROSS + j)
    for j in range(ACROSS):
        pair = get(UP * ACROSS + j // 2).astype(F32)
        half = pair[8:] if j % 2 else pair[:8]
        rows = jnp.concatenate([half, blank], axis=0).astype(BF16)
        out[first + UP * 16 : first + PADDED, j * 128 : (j + 1) * 128] = rows


def weights_kernel(gate_weight, up_weight, out, sems):
    fetch(sems, (gate_weight, out.at[:256]), (up_weight, out.at[256:]))


def spread_kernel(packed, out):
    for t in range(16):
        out[t] = packed[...]


def forward_kernel(place, rows, gu0, gu1, down0, down1, out, x_own, x_oth, wide, parts, sems):
    for t in range(16):
        wide[t * 88 : (t + 1) * 88, :] = rows[t].astype(F32)
    blank = jnp.zeros((PADDED - QUARTER, 128), F32)
    for far in range(2):
        for j in range(8):
            piece = jnp.concatenate([wide[pl.ds(far * 704 + j, QUARTER, stride=8), :], blank], axis=0)
            at = (j // 4 * 2 + j % 2) * 128
            ref = (x_own, x_oth)[j % 4 // 2]
            ref[far * PADDED : (far + 1) * PADDED, at : at + 128] = piece.astype(BF16)
    by_cols = (((1,), (0,)), ((), ()))
    by_rows = (((1,), (1,)), ((), ()))
    copies = []
    for m in range(3):
        cols, dims = (slice(256, 512), by_rows) if m == 2 else (slice(0, 256), by_cols)
        own, oth = (down0[...], down1[...]) if m == 2 else (gu[m * 256 : (m + 1) * 256, :] for gu in (gu0, gu1))
        total = lax.dot_general(x_own[:, cols], own, dims, preferred_element_type=F32)
        total = total + lax.dot_general(x_oth[:, cols], oth, dims, preferred_element_type=F32)
        put_tiles(parts, m, total[:PADDED], place[1])
        put_tiles(parts, m, total[PADDED:], 1 - place[1])
        here = pl.ds(m * SIZE, SIZE)
        copies.append(pltpu.make_async_copy(parts.at[:, here], out.at[:, here], sems.at[m]))
        copies[m].start()
    for copy in copies:
        copy.wait()


def activation_kernel(parts, acts):
    total = parts[0].astype(F32)
    for i in range(1, 16):
        total = total + parts[i].astype(F32)
    gate, up, back = total[:SIZE], total[SIZE : 2 * SIZE], total[2 * SIZE :]
    logistic = jax.nn.sigmoid(gate)
    hidden = (gate * logistic * up).astype(BF16)
    grad_gate_act = (back * up * logistic * (1.0 + gate * (1.0 - logistic))).astype(BF16)
    grad_up_act = (back * gate * logistic).astype(BF16)
    for i in range(8):
        acts[i, :SIZE, :] = grad_gate_act
        acts[i, SIZE : 2 * SIZE, :] = grad_up_act
        acts[i, 2 * SIZE :, :] = hidden


def token_grad_kernel(acts, gu0, gu1, gu2, gu3, out, gate_act, up_act, wide):
    get_tiles(acts, 0, gate_act, 0)
    get_tiles(acts, 1, up_act, 0)
    dims = (((1,), (1,)), ((), ()))
    for k, gu in enumerate((gu0, gu1, gu2, gu3)):
        part = lax.dot_general(gate_act[...], gu[:256, :], dims, preferred_element_type=F32)
        part = part + lax.dot_general(up_act[...], gu[256:, :], dims, preferred_element_type=F32)
        for j in range(2):
            wide[k // 2, pl.ds(k % 2 * 2 + j, QUARTER, stride=4), :] = tile(part[:QUARTER], j)
    for far in range(2):
        for i in range(8):
            out[far * 8 + i] = wide[far, i * 4 * ROWS : (i + 1) * 4 * ROWS, :].astype(BF16)


def token_sum_kernel(place, parts, out, total):
    odd = place[0] == 1
    acc = parts[0].astype(F32)
    for t in range(1, 16):
        acc = acc + parts[t].astype(F32)
    total[...] = acc
    pieces = [total[pl.ds(j, ROWS, stride=4), :] for j in range(4)]
    for j in range(4):
        out[:, j * 128 : (j + 1) * 128] = jnp.where(odd, pieces[(j + 2) % 4], pieces[j]).astype(BF16)


def weight_grad_kernel(x_own, x_got, acts0, acts1, acts2, acts3, grad_gate, grad_up, grad_down, x, act):
    contract_rows = (((0,), (0,)), ((), ()))
    for k in range(4):
        rows = slice(k // 2 * PADDED, (k // 2 + 1) * PADDED)
        x[k * PADDED : (k + 1) * PADDED, :] = (x_got if k % 2 else x_own)[rows, :]
    for m in range(3):
        for k, acts in enumerate((acts0, acts1, acts2, acts3)):
            get_tiles(acts, m, act, k * PADDED)
        if m < 2:
            out, left, right = (grad_gate, grad_up)[m], x[:, :256], act[...]
        else:
            out, left, right = grad_down, act[...], x[:, 256:]
        out[...] = lax.dot_general(left, right, contract_rows, preferred_element_type=F32).astype(BF16)


def copy_kernel(x, out):
    out[...] = x[...]


def after(x, *deps, flops=0):
    return call(copy_kernel, (shape(*x.shape, dtype=x.dtype),), (x,), deps=deps, flops=flops)[0]


def swap(axis, x):
    return lax.ppermute(x, axis, [(0, 1), (1, 0)])


def place_of(z, xh, core, xl, y):
    return (((z * 2 + xh) * 2 + core) * 2 + xl) * 8 + y


def permutation(to):
    grid = [(z, xh, c, xl, y) for z in range(8) for xh in range(2) for c in range(2) for xl in range(2) for y in range(8)]
    return [(place_of(*at), place_of(*to(*at))) for at in grid]


def per_device(tokens, cotangent, gate_weight, up_weight, down_weight):
    place = jnp.stack([lax.axis_index("core"), lax.axis_index("xh")]).astype(jnp.int32)
    there = permutation(lambda z, xh, c, xl, y: (4 * xl + y // 2, y % 2, c, xh ^ y % 2, z))
    home = [(b, a) for a, b in permutation(lambda z, xh, c, xl, y: (4 * xl + y // 2, xh, c, xh ^ y % 2, z))]

    packed, ready = call(
        pack_kernel,
        (shape(88, 128),),
        (place, tokens, cotangent),
        [pltpu.VMEM((88, 128), F32)],
        specs=[SMEM, VMEM, VMEM],
    )
    packed = lax.ppermute(packed, ALL, there)
    spread, _ = call(spread_kernel, (shape(16, 88, 128),), (packed,), flops=10**11)
    rows = lax.all_to_all(spread, TENSOR, 0, 0, tiled=True)
    gu0, _ = call(
        weights_kernel,
        (shape(512, 896),),
        (gate_weight, up_weight),
        [pltpu.SemaphoreType.DMA((2,))],
        specs=[HBM, HBM],
        deps=(ready,),
    )
    gu1, down1 = swap("core", gu0), swap("core", down_weight)

    parts, x_own, x_oth, ready = call(
        forward_kernel,
        (pltpu.HBM((16, 3 * SIZE, 128), BF16), shape(2 * PADDED, 512), shape(2 * PADDED, 512)),
        (place, rows, gu0, gu1, down_weight, down1),
        [
            pltpu.VMEM((16 * 88, 128), F32),
            pltpu.VMEM((16, 3 * SIZE, 128), BF16),
            pltpu.SemaphoreType.DMA((3,)),
        ],
        specs=[SMEM] + [VMEM] * 5,
        outs=[HBM, VMEM, VMEM],
        flops=12 * PADDED * 512 * 896,
    )
    parts = lax.all_to_all(parts, ("z", "xh"), 0, 0, tiled=True)
    x_got = swap("core", after(x_oth, ready))
    gu2 = swap("xh", after(gu0, ready))

    acts0, ready = call(activation_kernel, (shape(8, 3 * SIZE, 128),), (parts,))
    acts0 = lax.all_to_all(acts0, "z", 0, 0, tiled=True)
    gu3 = swap("core", after(gu2, ready, x_got))
    acts2 = swap("xh", acts0)

    token_parts, ready = call(
        token_grad_kernel,
        (shape(16, 4 * ROWS, 128),),
        (acts0, gu0, gu1, gu2, gu3),
        [
            pltpu.VMEM((PADDED, 896), BF16),
            pltpu.VMEM((PADDED, 896), BF16),
            pltpu.VMEM((2, 4 * QUARTER, 128), F32),
        ],
        flops=4 * PADDED * 1024 * 896,
    )
    token_parts = lax.all_to_all(token_parts, TENSOR, 0, 0, tiled=True)
    acts1 = swap("core", after(acts0, ready))

    grad_tokens, _ = call(
        token_sum_kernel,
        (shape(ROWS, 512),),
        (place, token_parts),
        [pltpu.VMEM((4 * ROWS, 128), F32)],
        specs=[SMEM, VMEM],
    )
    grad_tokens = after(lax.ppermute(grad_tokens, ALL, home), flops=10**11)
    acts3 = swap("core", acts2)

    grad_gate, grad_up, grad_down, _ = call(
        weight_grad_kernel,
        (shape(256, 896), shape(256, 896), shape(896, 256)),
        (x_own, x_got, acts0, acts1, acts2, acts3),
        [pltpu.VMEM((4 * PADDED, 512), BF16), pltpu.VMEM((4 * PADDED, 896), BF16)],
        flops=6 * 4 * PADDED * 256 * 896,
    )
    return (grad_tokens, grad_gate, grad_up, grad_down)


def solution(mesh):
    chips = Mesh(mesh.devices.reshape(8, 2, 2, 2, 8), ALL)
    rows, cols = P(FSDP, TENSOR), P(TENSOR, FSDP)
    return jax.shard_map(
        per_device,
        mesh=chips,
        in_specs=(rows, rows, rows, rows, cols),
        out_specs=(rows, rows, rows, cols),
        check_vma=False,
    )
```

```python
import math

import jax
import jax.numpy as jnp
from jax import lax
from jax.experimental import pallas as pl
from jax.experimental.pallas import tpu as pltpu
from jax.sharding import Mesh
from jax.sharding import PartitionSpec as P

F32, BF16 = jnp.float32, jnp.bfloat16
ALL = ("z", "xh", "core", "xl", "y")
FSDP = ("z", "xh", "core")
TENSOR = ("xl", "y")

ROWS, QUARTER, PADDED = 11, 88, 96
UP, ACROSS, PER = 5, 7, 5
SIZE = PER * 16
VMEM = pl.BlockSpec(memory_space=pltpu.VMEM)
HBM = pl.BlockSpec(memory_space=pltpu.HBM)
SMEM = pl.BlockSpec(memory_space=pltpu.SMEM)
PARAMS = pltpu.CompilerParams(vmem_limit_bytes=20 * 1024 * 1024)


def call(kernel, out_shape, inputs, scratch=(), specs=None, flops=0, deps=(), outs=None):
    moved = sum(x.size * x.dtype.itemsize for x in inputs)
    moved += sum(math.prod(s.shape) * s.dtype.itemsize for s in out_shape)
    n, m = len(inputs), len(out_shape)

    def body(*refs):
        rest = refs[n + len(deps) :]
        rest[m][...] = jnp.zeros((8, 128), F32)
        kernel(*refs[:n], *rest[:m], *rest[m + 1 :])

    return pl.pallas_call(
        body,
        out_shape=(*out_shape, shape(8, 128, dtype=F32)),
        in_specs=list(specs or [VMEM] * n) + [VMEM] * len(deps),
        out_specs=list(outs or [VMEM] * m) + [VMEM],
        scratch_shapes=list(scratch),
        compiler_params=PARAMS,
        cost_estimate=pl.CostEstimate(flops=flops, bytes_accessed=moved, transcendentals=0),
    )(*inputs, *deps)


def shape(*dims, dtype=BF16):
    return jax.ShapeDtypeStruct(dims, dtype)


def tile(ref_or_value, j):
    return ref_or_value[:, j * 128 : (j + 1) * 128]


def fetch(sems, *pairs):
    copies = [pltpu.make_async_copy(source, to, sems.at[i]) for i, (source, to) in enumerate(pairs)]
    for copy in copies:
        copy.start()
    for copy in copies:
        copy.wait()


def pack_kernel(place, tok_hbm, cot_hbm, out, wide, tok, cot, sems):
    fetch(sems, (tok_hbm, tok), (cot_hbm, cot))
    odd = place[0] == 1
    for base, ref in ((0, tok), (4, cot)):
        rows = ref[...].astype(F32)
        for j in range(4):
            piece = jnp.where(odd, tile(rows, (j + 2) % 4), tile(rows, j))
            wide[pl.ds(base + j, ROWS, stride=8), :] = piece
    out[...] = wide[...].astype(BF16)


def put_tiles(out, m, value, half):
    def put(slot, rows):
        row = m * SIZE + slot % PER * 16
        out[slot // PER * 2 + half, row : row + 16, :] = rows.astype(BF16)

    blank = jnp.zeros((8, 128), F32)
    for i in range(UP):
        for j in range(ACROSS):
            put(i * ACROSS + j, tile(value[i * 16 : (i + 1) * 16], j))
    last = [tile(value[UP * 16 : QUARTER], j) for j in range(ACROSS)] + [blank] * 3
    for j in range(0, 10, 2):
        put(UP * ACROSS + j // 2, jnp.concatenate([last[j], last[j + 1]], axis=0))


def get_tiles(ref, m, out, first):
    def get(slot):
        row = m * SIZE + slot % PER * 16
        return ref[slot // PER, row : row + 16, :]

    blank = jnp.zeros((8, 128), F32)
    for i in range(UP):
        for j in range(ACROSS):
            out[first + i * 16 : first + (i + 1) * 16, j * 128 : (j + 1) * 128] = get(i * ACROSS + j)
    for j in range(ACROSS):
        pair = get(UP * ACROSS + j // 2).astype(F32)
        half = pair[8:] if j % 2 else pair[:8]
        rows = jnp.concatenate([half, blank], axis=0).astype(BF16)
        out[first + UP * 16 : first + PADDED, j * 128 : (j + 1) * 128] = rows


def weights_kernel(gate_weight, up_weight, out, sems):
    fetch(sems, (gate_weight, out.at[:256]), (up_weight, out.at[256:]))


def spread_kernel(packed, out):
    for t in range(16):
        out[t] = packed[...]


def forward_kernel(
    place, rows, gu0, gu1, down0, down1, out, own_out, oth_out, wide, parts, x_own, x_oth, sems
):
    for t in range(16):
        wide[t * 88 : (t + 1) * 88, :] = rows[t].astype(F32)
    blank = jnp.zeros((PADDED - QUARTER, 128), F32)
    for far in range(2):
        for j in range(8):
            piece = jnp.concatenate([wide[pl.ds(far * 704 + j, QUARTER, stride=8), :], blank], axis=0)
            at = (j // 4 * 2 + j % 2) * 128
            ref = (x_own, x_oth)[j % 4 // 2]
            ref[far * PADDED : (far + 1) * PADDED, at : at + 128] = piece.astype(BF16)
    by_cols = (((1,), (0,)), ((), ()))
    by_rows = (((1,), (1,)), ((), ()))
    copies = [
        pltpu.make_async_copy(x_own, own_out, sems.at[3]),
        pltpu.make_async_copy(x_oth, oth_out, sems.at[4]),
    ]
    for copy in copies:
        copy.start()
    for m in range(3):
        cols, dims = (slice(256, 512), by_rows) if m == 2 else (slice(0, 256), by_cols)
        own, oth = (down0[...], down1[...]) if m == 2 else (gu[m * 256 : (m + 1) * 256, :] for gu in (gu0, gu1))
        total = lax.dot_general(x_own[:, cols], own, dims, preferred_element_type=F32)
        total = total + lax.dot_general(x_oth[:, cols], oth, dims, preferred_element_type=F32)
        put_tiles(parts, m, total[:PADDED], place[1])
        put_tiles(parts, m, total[PADDED:], 1 - place[1])
        here = pl.ds(m * SIZE, SIZE)
        copies.append(pltpu.make_async_copy(parts.at[:, here], out.at[:, here], sems.at[m]))
        copies[-1].start()
    for copy in copies:
        copy.wait()


def activation_kernel(parts, acts):
    total = parts[0].astype(F32)
    for i in range(1, 16):
        total = total + parts[i].astype(F32)
    gate, up, back = total[:SIZE], total[SIZE : 2 * SIZE], total[2 * SIZE :]
    logistic = jax.nn.sigmoid(gate)
    hidden = (gate * logistic * up).astype(BF16)
    grad_gate_act = (back * up * logistic * (1.0 + gate * (1.0 - logistic))).astype(BF16)
    grad_up_act = (back * gate * logistic).astype(BF16)
    for i in range(8):
        acts[i, :SIZE, :] = grad_gate_act
        acts[i, SIZE : 2 * SIZE, :] = grad_up_act
        acts[i, 2 * SIZE :, :] = hidden


def token_grad_kernel(acts, gu0, gu1, gu2, gu3, out, gate_act, up_act, wide):
    get_tiles(acts, 0, gate_act, 0)
    get_tiles(acts, 1, up_act, 0)
    dims = (((1,), (1,)), ((), ()))
    for k, gu in enumerate((gu0, gu1, gu2, gu3)):
        part = lax.dot_general(gate_act[...], gu[:256, :], dims, preferred_element_type=F32)
        part = part + lax.dot_general(up_act[...], gu[256:, :], dims, preferred_element_type=F32)
        for j in range(2):
            wide[k // 2, pl.ds(k % 2 * 2 + j, QUARTER, stride=4), :] = tile(part[:QUARTER], j)
    for far in range(2):
        for i in range(8):
            out[far * 8 + i] = wide[far, i * 4 * ROWS : (i + 1) * 4 * ROWS, :].astype(BF16)


def token_sum_kernel(place, parts, out, total):
    odd = place[0] == 1
    acc = parts[0].astype(F32)
    for t in range(1, 16):
        acc = acc + parts[t].astype(F32)
    total[...] = acc
    pieces = [total[pl.ds(j, ROWS, stride=4), :] for j in range(4)]
    for j in range(4):
        out[:, j * 128 : (j + 1) * 128] = jnp.where(odd, pieces[(j + 2) % 4], pieces[j]).astype(BF16)


def weight_grad_kernel(x_own, x_got, acts0, acts1, acts2, acts3, grad_gate, grad_up, grad_down, x, act):
    contract_rows = (((0,), (0,)), ((), ()))
    for k in range(4):
        rows = slice(k // 2 * PADDED, (k // 2 + 1) * PADDED)
        x[k * PADDED : (k + 1) * PADDED, :] = (x_got if k % 2 else x_own)[rows, :]
    for m in range(3):
        for k, acts in enumerate((acts0, acts1, acts2, acts3)):
            get_tiles(acts, m, act, k * PADDED)
        if m < 2:
            out, left, right = (grad_gate, grad_up)[m], x[:, :256], act[...]
        else:
            out, left, right = grad_down, act[...], x[:, 256:]
        out[...] = lax.dot_general(left, right, contract_rows, preferred_element_type=F32).astype(BF16)


def copy_kernel(x, out):
    out[...] = x[...]


def after(x, *deps):
    return call(copy_kernel, (shape(*x.shape, dtype=x.dtype),), (x,), deps=deps)[0]


def in_hbm(x):
    return pltpu.with_memory_space_constraint(x, pltpu.HBM)


def swap(axis, x):
    return lax.ppermute(x, axis, [(0, 1), (1, 0)])


def place_of(z, xh, core, xl, y):
    return (((z * 2 + xh) * 2 + core) * 2 + xl) * 8 + y


def permutation(to):
    grid = [(z, xh, c, xl, y) for z in range(8) for xh in range(2) for c in range(2) for xl in range(2) for y in range(8)]
    return [(place_of(*at), place_of(*to(*at))) for at in grid]


def per_device(tokens, cotangent, gate_weight, up_weight, down_weight):
    place = jnp.stack([lax.axis_index("core"), lax.axis_index("xh")]).astype(jnp.int32)
    there = permutation(lambda z, xh, c, xl, y: (4 * xl + y // 2, y % 2, c, xh ^ y % 2, z))
    home = [(b, a) for a, b in permutation(lambda z, xh, c, xl, y: (4 * xl + y // 2, xh, c, xh ^ y % 2, z))]

    packed, ready0 = call(
        pack_kernel,
        (shape(88, 128),),
        (place, in_hbm(tokens), in_hbm(cotangent)),
        [
            pltpu.VMEM((88, 128), F32),
            pltpu.VMEM((ROWS, 512), BF16),
            pltpu.VMEM((ROWS, 512), BF16),
            pltpu.SemaphoreType.DMA((2,)),
        ],
        specs=[SMEM, HBM, HBM],
    )
    packed = lax.ppermute(packed, ALL, there)
    spread, _ = call(spread_kernel, (shape(16, 88, 128),), (packed,), flops=10**11)
    rows = lax.all_to_all(spread, TENSOR, 0, 0, tiled=True)
    gu0, _ = call(
        weights_kernel,
        (shape(512, 896),),
        (in_hbm(gate_weight), in_hbm(up_weight)),
        [pltpu.SemaphoreType.DMA((2,))],
        specs=[HBM, HBM],
        deps=(ready0,),
    )
    gu1, down1 = swap("core", gu0), swap("core", down_weight)

    parts, x_own, x_oth, ready = call(
        forward_kernel,
        (pltpu.HBM((16, 3 * SIZE, 128), BF16), *[pltpu.HBM((2 * PADDED, 512), BF16)] * 2),
        (place, rows, gu0, gu1, down_weight, down1),
        [
            pltpu.VMEM((16 * 88, 128), F32),
            pltpu.VMEM((16, 3 * SIZE, 128), BF16),
            pltpu.VMEM((2 * PADDED, 512), BF16),
            pltpu.VMEM((2 * PADDED, 512), BF16),
            pltpu.SemaphoreType.DMA((5,)),
        ],
        specs=[SMEM] + [VMEM] * 5,
        outs=[HBM] * 3,
    )
    parts = lax.all_to_all(parts, ("z", "xh"), 0, 0, tiled=True)
    x_got = swap("core", after(x_oth, ready))
    gu2 = swap("xh", after(gu0, ready))

    acts0, ready = call(activation_kernel, (shape(8, 3 * SIZE, 128),), (parts,))
    acts0 = lax.all_to_all(acts0, "z", 0, 0, tiled=True)
    gu3 = swap("core", after(gu2, ready, x_got))
    token_parts, ready = call(
        token_grad_kernel,
        (shape(16, 4 * ROWS, 128),),
        (acts0, gu0, gu1, gu2, gu3),
        [
            pltpu.VMEM((PADDED, 896), BF16),
            pltpu.VMEM((PADDED, 896), BF16),
            pltpu.VMEM((2, 4 * QUARTER, 128), F32),
        ],
    )
    token_parts = lax.all_to_all(token_parts, TENSOR, 0, 0, tiled=True)
    acts2 = swap("xh", acts0)
    acts1 = swap("core", acts0)
    acts3 = swap("core", acts2)

    grad_tokens, _ = call(
        token_sum_kernel,
        (shape(ROWS, 512),),
        (place, token_parts),
        [pltpu.VMEM((4 * ROWS, 128), F32)],
        specs=[SMEM, VMEM],
        flops=10**11,
    )
    grad_tokens = lax.ppermute(grad_tokens, ALL, home)

    grad_gate, grad_up, grad_down, ready = call(
        weight_grad_kernel,
        (shape(256, 896), shape(256, 896), shape(896, 256)),
        (x_own, x_got, acts0, acts1, acts2, acts3),
        [pltpu.VMEM((4 * PADDED, 512), BF16), pltpu.VMEM((4 * PADDED, 896), BF16)],
    )
    return (after(grad_tokens, ready), grad_gate, grad_up, grad_down)


def solution(mesh):
    chips = Mesh(mesh.devices.reshape(8, 2, 2, 2, 8), ALL)
    rows, cols = P(FSDP, TENSOR), P(TENSOR, FSDP)
    return jax.shard_map(
        per_device,
        mesh=chips,
        in_specs=(rows, rows, rows, rows, cols),
        out_specs=(rows, rows, rows, cols),
        check_vma=False,
    )
```

```python
import math

import jax
import jax.numpy as jnp
from jax import lax
from jax.experimental import pallas as pl
from jax.experimental.pallas import tpu as pltpu
from jax.sharding import Mesh
from jax.sharding import PartitionSpec as P

F32, BF16 = jnp.float32, jnp.bfloat16
ALL = ("z", "xh", "core", "xl", "y")
FSDP = ("z", "xh", "core")
TENSOR = ("xl", "y")

ROWS, QUARTER, PADDED = 11, 88, 96
UP, ACROSS, PER = 5, 7, 5
SIZE = PER * 16
VMEM = pl.BlockSpec(memory_space=pltpu.VMEM)
HBM = pl.BlockSpec(memory_space=pltpu.HBM)
SMEM = pl.BlockSpec(memory_space=pltpu.SMEM)
PARAMS = pltpu.CompilerParams(vmem_limit_bytes=20 * 1024 * 1024)


def call(kernel, out_shape, inputs, scratch=(), specs=None, flops=0, deps=(), outs=None):
    moved = sum(x.size * x.dtype.itemsize for x in inputs)
    moved += sum(math.prod(s.shape) * s.dtype.itemsize for s in out_shape)
    n, m = len(inputs), len(out_shape)

    def body(*refs):
        rest = refs[n + len(deps) :]
        rest[m][...] = jnp.zeros((8, 128), F32)
        kernel(*refs[:n], *rest[:m], *rest[m + 1 :])

    return pl.pallas_call(
        body,
        out_shape=(*out_shape, shape(8, 128, dtype=F32)),
        in_specs=list(specs or [VMEM] * n) + [VMEM] * len(deps),
        out_specs=list(outs or [VMEM] * m) + [VMEM],
        scratch_shapes=list(scratch),
        compiler_params=PARAMS,
        cost_estimate=pl.CostEstimate(flops=flops, bytes_accessed=moved, transcendentals=0),
    )(*inputs, *deps)


def shape(*dims, dtype=BF16):
    return jax.ShapeDtypeStruct(dims, dtype)


def tile(ref_or_value, j):
    return ref_or_value[:, j * 128 : (j + 1) * 128]


def fetch(sems, *pairs):
    copies = [pltpu.make_async_copy(source, to, sems.at[i]) for i, (source, to) in enumerate(pairs)]
    for copy in copies:
        copy.start()
    for copy in copies:
        copy.wait()


def pack_kernel(place, tok_hbm, cot_hbm, out, wide, tok, cot, sems):
    fetch(sems, (tok_hbm, tok), (cot_hbm, cot))
    odd = place[0] == 1
    for base, ref in ((0, tok), (4, cot)):
        rows = ref[...].astype(F32)
        for j in range(4):
            piece = jnp.where(odd, tile(rows, (j + 2) % 4), tile(rows, j))
            wide[pl.ds(base + j, ROWS, stride=8), :] = piece
    out[...] = wide[...].astype(BF16)


def put_tiles(out, m, value, half):
    def put(slot, rows):
        row = m * SIZE + slot % PER * 16
        out[slot // PER * 2 + half, row : row + 16, :] = rows.astype(BF16)

    blank = jnp.zeros((8, 128), F32)
    for i in range(UP):
        for j in range(ACROSS):
            put(i * ACROSS + j, tile(value[i * 16 : (i + 1) * 16], j))
    last = [tile(value[UP * 16 : QUARTER], j) for j in range(ACROSS)] + [blank] * 3
    for j in range(0, 10, 2):
        put(UP * ACROSS + j // 2, jnp.concatenate([last[j], last[j + 1]], axis=0))


def get_tiles(ref, m, out, first):
    def get(slot):
        row = m * SIZE + slot % PER * 16
        return ref[slot // PER, row : row + 16, :]

    blank = jnp.zeros((8, 128), F32)
    for i in range(UP):
        for j in range(ACROSS):
            out[first + i * 16 : first + (i + 1) * 16, j * 128 : (j + 1) * 128] = get(i * ACROSS + j)
    for j in range(ACROSS):
        pair = get(UP * ACROSS + j // 2).astype(F32)
        half = pair[8:] if j % 2 else pair[:8]
        rows = jnp.concatenate([half, blank], axis=0).astype(BF16)
        out[first + UP * 16 : first + PADDED, j * 128 : (j + 1) * 128] = rows


def weights_kernel(gate_weight, up_weight, out, sems):
    fetch(sems, (gate_weight, out.at[:256]), (up_weight, out.at[256:]))


def spread_kernel(packed, out):
    for t in range(16):
        out[t] = packed[...]


def came_from(base, i):
    return lax.rem(base - i + 8, 8)


def transpose_kernel(gu, out):
    out[:, :256] = gu[:256, :].T
    out[:, 256:] = gu[256:, :].T


def forward_kernel(
    place, rows, gu0, gu1, down0, down1, out, own_out, oth_out, wide, parts, x_own, x_oth, sems
):
    for far in range(2):
        for i in range(8):
            at = (far * 8 + i) * 88
            wide[at : at + 88, :] = rows[far * 8 + came_from(place[2], i)].astype(F32)
    blank = jnp.zeros((PADDED - QUARTER, 128), F32)
    for far in range(2):
        for j in range(8):
            piece = jnp.concatenate([wide[pl.ds(far * 704 + j, QUARTER, stride=8), :], blank], axis=0)
            at = (j // 4 * 2 + j % 2) * 128
            ref = (x_own, x_oth)[j % 4 // 2]
            ref[far * PADDED : (far + 1) * PADDED, at : at + 128] = piece.astype(BF16)
    by_cols = (((1,), (0,)), ((), ()))
    by_rows = (((1,), (1,)), ((), ()))
    copies = [
        pltpu.make_async_copy(x_own, own_out, sems.at[3]),
        pltpu.make_async_copy(x_oth, oth_out, sems.at[4]),
    ]
    for copy in copies:
        copy.start()
    for m in range(3):
        cols, dims = (slice(256, 512), by_rows) if m == 2 else (slice(0, 256), by_cols)
        own, oth = (down0[...], down1[...]) if m == 2 else (gu[m * 256 : (m + 1) * 256, :] for gu in (gu0, gu1))
        total = lax.dot_general(x_own[:, cols], own, dims, preferred_element_type=F32)
        total = total + lax.dot_general(x_oth[:, cols], oth, dims, preferred_element_type=F32)
        put_tiles(parts, m, total[:PADDED], place[1])
        put_tiles(parts, m, total[PADDED:], 1 - place[1])
        here = pl.ds(m * SIZE, SIZE)
        copies.append(pltpu.make_async_copy(parts.at[:, here], out.at[:, here], sems.at[m]))
        copies[-1].start()
    for copy in copies:
        copy.wait()


def activation_kernel(parts, acts):
    total = parts[0].astype(F32)
    for i in range(1, 16):
        total = total + parts[i].astype(F32)
    gate, up, back = total[:SIZE], total[SIZE : 2 * SIZE], total[2 * SIZE :]
    logistic = jax.nn.sigmoid(gate)
    hidden = (gate * logistic * up).astype(BF16)
    grad_gate_act = (back * up * logistic * (1.0 + gate * (1.0 - logistic))).astype(BF16)
    grad_up_act = (back * gate * logistic).astype(BF16)
    for i in range(8):
        acts[i, :SIZE, :] = grad_gate_act
        acts[i, SIZE : 2 * SIZE, :] = grad_up_act
        acts[i, 2 * SIZE :, :] = hidden


def token_grad_kernel(
    place, acts, gu1, gu3, gu0_hbm, gu2_hbm, out, gate_act, up_act, wide, gu0, gu2, sems
):
    copies = {0: pltpu.make_async_copy(gu0_hbm, gu0, sems.at[0]), 2: pltpu.make_async_copy(gu2_hbm, gu2, sems.at[1])}
    for copy in copies.values():
        copy.start()
    get_tiles(acts, 0, gate_act, 0)
    get_tiles(acts, 1, up_act, 0)
    for k, gu in ((1, gu1), (3, gu3), (0, gu0), (2, gu2)):
        if k in copies:
            copies[k].wait()
        part = jnp.dot(gate_act[...], gu[:, :256], preferred_element_type=F32)
        part = part + jnp.dot(up_act[...], gu[:, 256:], preferred_element_type=F32)
        for j in range(2):
            wide[k // 2, pl.ds(k % 2 * 2 + j, QUARTER, stride=4), :] = tile(part[:QUARTER], j)
    for far in range(2):
        for i in range(8):
            rows = wide[far, i * 4 * ROWS : (i + 1) * 4 * ROWS, :]
            out[far * 8 + came_from(place[2 + far], i)] = rows.astype(BF16)


def token_sum_kernel(place, parts, out, total):
    odd = place[0] == 1
    acc = parts[0].astype(F32)
    for t in range(1, 16):
        acc = acc + parts[t].astype(F32)
    total[...] = acc
    pieces = [total[pl.ds(j, ROWS, stride=4), :] for j in range(4)]
    for j in range(4):
        out[:, j * 128 : (j + 1) * 128] = jnp.where(odd, pieces[(j + 2) % 4], pieces[j]).astype(BF16)


def weight_grad_kernel(x_own, x_got, acts0, acts1, acts2, acts3, grad_gate, grad_up, grad_down, x, act):
    contract_rows = (((0,), (0,)), ((), ()))
    for k in range(4):
        rows = slice(k // 2 * PADDED, (k // 2 + 1) * PADDED)
        x[k * PADDED : (k + 1) * PADDED, :] = (x_got if k % 2 else x_own)[rows, :]
    for m in range(3):
        for k, acts in enumerate((acts0, acts1, acts2, acts3)):
            get_tiles(acts, m, act, k * PADDED)
        if m < 2:
            out, left, right = (grad_gate, grad_up)[m], x[:, :256], act[...]
        else:
            out, left, right = grad_down, act[...], x[:, 256:]
        out[...] = lax.dot_general(left, right, contract_rows, preferred_element_type=F32).astype(BF16)


def copy_kernel(x, out):
    out[...] = x[...]


def after(x, *deps):
    return call(copy_kernel, (shape(*x.shape, dtype=x.dtype),), (x,), deps=deps)[0]


def after_in_hbm(x, dep):
    return pl.pallas_call(
        lambda *refs: None,
        out_shape=pltpu.HBM(x.shape, x.dtype),
        in_specs=[HBM, VMEM],
        out_specs=HBM,
        input_output_aliases={0: 0},
        compiler_params=PARAMS,
    )(in_hbm(x), dep)


def in_hbm(x):
    return pltpu.with_memory_space_constraint(x, pltpu.HBM)


def swap(axis, x):
    return lax.ppermute(x, axis, [(0, 1), (1, 0)])


def place_of(z, xh, core, xl, y):
    return (((z * 2 + xh) * 2 + core) * 2 + xl) * 8 + y


def permutation(to):
    grid = [(z, xh, c, xl, y) for z in range(8) for xh in range(2) for c in range(2) for xl in range(2) for y in range(8)]
    return [(place_of(*at), place_of(*to(*at))) for at in grid]


def per_device(tokens, cotangent, gate_weight, up_weight, down_weight):
    z, xh, core = (lax.axis_index(axis) for axis in FSDP)
    base = z + 4 + z % 4 * 2
    place = jnp.stack([core, xh, (base + xh) % 8, (base + 1 - xh) % 8]).astype(jnp.int32)
    def chip(z, xl, y):
        return 4 * xl + y // 2, (y + 4 - z + 4 * xl + y // 2) % 8

    def forth(z, xh, c, xl, y):
        to, row = chip(z, xl, y)
        return to, y % 2, c, xh ^ y % 2, row

    def back(z, xh, c, xl, y):
        to, row = chip(z, xl, y)
        return to, xh, c, xh ^ y % 2, row

    there = permutation(forth)
    home = [(b, a) for a, b in permutation(back)]

    packed, ready0 = call(
        pack_kernel,
        (shape(88, 128),),
        (place, in_hbm(tokens), in_hbm(cotangent)),
        [
            pltpu.VMEM((88, 128), F32),
            pltpu.VMEM((ROWS, 512), BF16),
            pltpu.VMEM((ROWS, 512), BF16),
            pltpu.SemaphoreType.DMA((2,)),
        ],
        specs=[SMEM, HBM, HBM],
    )
    packed = lax.ppermute(packed, ALL, there)
    spread, _ = call(spread_kernel, (shape(16, 88, 128),), (packed,), flops=10**11)
    rows = lax.all_to_all(spread, TENSOR, 0, 0, tiled=True)
    gu0, _ = call(
        weights_kernel,
        (shape(512, 896),),
        (in_hbm(gate_weight), in_hbm(up_weight)),
        [pltpu.SemaphoreType.DMA((2,))],
        specs=[HBM, HBM],
        deps=(ready0,),
    )
    gu1, down1 = swap("core", gu0), swap("core", down_weight)

    parts, x_own, x_oth, ready = call(
        forward_kernel,
        (pltpu.HBM((16, 3 * SIZE, 128), BF16), *[pltpu.HBM((2 * PADDED, 512), BF16)] * 2),
        (place, rows, gu0, gu1, down_weight, down1),
        [
            pltpu.VMEM((16 * 88, 128), F32),
            pltpu.VMEM((16, 3 * SIZE, 128), BF16),
            pltpu.VMEM((2 * PADDED, 512), BF16),
            pltpu.VMEM((2 * PADDED, 512), BF16),
            pltpu.SemaphoreType.DMA((5,)),
        ],
        specs=[SMEM] + [VMEM] * 5,
        outs=[HBM] * 3,
    )
    parts = lax.all_to_all(parts, ("z", "xh"), 0, 0, tiled=True)
    x_got = swap("core", after(x_oth, ready))
    t0, _ = call(transpose_kernel, (shape(896, 512),), (gu0,), deps=(ready,))
    t2 = swap("xh", t0)

    acts0, ready = call(activation_kernel, (shape(8, 3 * SIZE, 128),), (parts,))
    acts0 = lax.all_to_all(acts0, "z", 0, 0, tiled=True)
    t1, ready = call(transpose_kernel, (shape(896, 512),), (gu1,), deps=(ready,))
    t2 = after_in_hbm(t2, ready)
    t3 = swap("core", t2)
    token_parts, ready = call(
        token_grad_kernel,
        (shape(16, 4 * ROWS, 128),),
        (place, acts0, t1, t3, in_hbm(t0), in_hbm(t2)),
        [
            pltpu.VMEM((PADDED, 896), BF16),
            pltpu.VMEM((PADDED, 896), BF16),
            pltpu.VMEM((2, 4 * QUARTER, 128), F32),
            pltpu.VMEM((896, 512), BF16),
            pltpu.VMEM((896, 512), BF16),
            pltpu.SemaphoreType.DMA((2,)),
        ],
        specs=[SMEM] + [VMEM] * 3 + [HBM] * 2,
        deps=(x_got,),
    )
    token_parts = lax.all_to_all(token_parts, TENSOR, 0, 0, tiled=True)
    acts2 = swap("xh", acts0)
    acts1 = swap("core", acts0)
    acts3 = swap("core", acts2)

    grad_tokens, _ = call(
        token_sum_kernel,
        (shape(ROWS, 512),),
        (place, token_parts),
        [pltpu.VMEM((4 * ROWS, 128), F32)],
        specs=[SMEM, VMEM],
        flops=10**11,
    )
    grad_tokens = lax.ppermute(grad_tokens, ALL, home)

    grad_gate, grad_up, grad_down, ready = call(
        weight_grad_kernel,
        (shape(256, 896), shape(256, 896), shape(896, 256)),
        (x_own, x_got, acts0, acts1, acts2, acts3),
        [pltpu.VMEM((4 * PADDED, 512), BF16), pltpu.VMEM((4 * PADDED, 896), BF16)],
    )
    return (after(grad_tokens, ready), grad_gate, grad_up, grad_down)


def solution(mesh):
    chips = Mesh(mesh.devices.reshape(8, 2, 2, 2, 8), ALL)
    rows, cols = P(FSDP, TENSOR), P(TENSOR, FSDP)
    return jax.shard_map(
        per_device,
        mesh=chips,
        in_specs=(rows, rows, rows, rows, cols),
        out_specs=(rows, rows, rows, cols),
        check_vma=False,
    )
```

```python
import math

import jax
import jax.numpy as jnp
from jax import lax
from jax.experimental import pallas as pl
from jax.experimental.pallas import tpu as pltpu
from jax.sharding import Mesh
from jax.sharding import PartitionSpec as P

F32, BF16 = jnp.float32, jnp.bfloat16
ALL = ("z", "xh", "core", "xl", "y")
FSDP = ("z", "xh", "core")
TENSOR = ("xl", "y")

ROWS, QUARTER, PADDED = 11, 88, 96
UP, ACROSS, PER = 5, 7, 5
SIZE = PER * 16
VMEM = pl.BlockSpec(memory_space=pltpu.VMEM)
HBM = pl.BlockSpec(memory_space=pltpu.HBM)
SMEM = pl.BlockSpec(memory_space=pltpu.SMEM)
PARAMS = pltpu.CompilerParams(vmem_limit_bytes=20 * 1024 * 1024)


def call(kernel, out_shape, inputs, scratch=(), specs=None, flops=0, deps=(), outs=None):
    moved = sum(x.size * x.dtype.itemsize for x in inputs)
    moved += sum(math.prod(s.shape) * s.dtype.itemsize for s in out_shape)
    n, m = len(inputs), len(out_shape)

    def body(*refs):
        rest = refs[n + len(deps) :]
        rest[m][...] = jnp.zeros((8, 128), F32)
        kernel(*refs[:n], *rest[:m], *rest[m + 1 :])

    return pl.pallas_call(
        body,
        out_shape=(*out_shape, shape(8, 128, dtype=F32)),
        in_specs=list(specs or [VMEM] * n) + [VMEM] * len(deps),
        out_specs=list(outs or [VMEM] * m) + [VMEM],
        scratch_shapes=list(scratch),
        compiler_params=PARAMS,
        cost_estimate=pl.CostEstimate(flops=flops, bytes_accessed=moved, transcendentals=0),
    )(*inputs, *deps)


def shape(*dims, dtype=BF16):
    return jax.ShapeDtypeStruct(dims, dtype)


def tile(ref_or_value, j):
    return ref_or_value[:, j * 128 : (j + 1) * 128]


def fetch(sems, *pairs):
    copies = [pltpu.make_async_copy(source, to, sems.at[i]) for i, (source, to) in enumerate(pairs)]
    for copy in copies:
        copy.start()
    for copy in copies:
        copy.wait()


def pack_kernel(place, tok_hbm, cot_hbm, out, wide, tok, cot, sems):
    fetch(sems, (tok_hbm, tok), (cot_hbm, cot))
    odd = place[0] == 1
    for base, ref in ((0, tok), (4, cot)):
        rows = ref[...].astype(F32)
        for j in range(4):
            piece = jnp.where(odd, tile(rows, (j + 2) % 4), tile(rows, j))
            wide[pl.ds(base + j, ROWS, stride=8), :] = piece
    out[...] = wide[...].astype(BF16)


def put_tiles(out, m, value, half):
    def put(slot, rows):
        row = m * SIZE + slot % PER * 16
        out[slot // PER * 2 + half, row : row + 16, :] = rows.astype(BF16)

    blank = jnp.zeros((8, 128), F32)
    for i in range(UP):
        for j in range(ACROSS):
            put(i * ACROSS + j, tile(value[i * 16 : (i + 1) * 16], j))
    last = [tile(value[UP * 16 : QUARTER], j) for j in range(ACROSS)] + [blank] * 3
    for j in range(0, 10, 2):
        put(UP * ACROSS + j // 2, jnp.concatenate([last[j], last[j + 1]], axis=0))


def get_tiles(ref, m, out, first):
    def get(slot):
        row = m * SIZE + slot % PER * 16
        return ref[slot // PER, row : row + 16, :]

    blank = jnp.zeros((8, 128), F32)
    for i in range(UP):
        for j in range(ACROSS):
            out[first + i * 16 : first + (i + 1) * 16, j * 128 : (j + 1) * 128] = get(i * ACROSS + j)
    for j in range(ACROSS):
        pair = get(UP * ACROSS + j // 2).astype(F32)
        half = pair[8:] if j % 2 else pair[:8]
        rows = jnp.concatenate([half, blank], axis=0).astype(BF16)
        out[first + UP * 16 : first + PADDED, j * 128 : (j + 1) * 128] = rows


def weights_kernel(gate_weight, up_weight, out, sems):
    fetch(sems, (gate_weight, out.at[:256]), (up_weight, out.at[256:]))


def spread_kernel(packed, out):
    for t in range(16):
        out[t] = packed[...]


def came_from(base, i):
    return lax.rem(base - i + 8, 8)


def transpose_kernel(gu, out):
    out[:, :256] = gu[:256, :].T
    out[:, 256:] = gu[256:, :].T


def forward_kernel(
    place, rows, gu0, gu1, down0, down1, out, own_out, oth_out, wide, parts, x_own, x_oth, sems
):
    for far in range(2):
        for i in range(8):
            at = (far * 8 + i) * 88
            wide[at : at + 88, :] = rows[lax.rem(far + place[4], 2) * 8 + came_from(place[2], i)].astype(F32)
    blank = jnp.zeros((PADDED - QUARTER, 128), F32)
    for far in range(2):
        for j in range(8):
            piece = jnp.concatenate([wide[pl.ds(far * 704 + j, QUARTER, stride=8), :], blank], axis=0)
            at = (j // 4 * 2 + j % 2) * 128
            ref = (x_own, x_oth)[j % 4 // 2]
            ref[far * PADDED : (far + 1) * PADDED, at : at + 128] = piece.astype(BF16)
    by_cols = (((1,), (0,)), ((), ()))
    by_rows = (((1,), (1,)), ((), ()))
    copies = [
        pltpu.make_async_copy(x_own, own_out, sems.at[3]),
        pltpu.make_async_copy(x_oth, oth_out, sems.at[4]),
    ]
    for copy in copies:
        copy.start()
    for m in range(3):
        cols, dims = (slice(256, 512), by_rows) if m == 2 else (slice(0, 256), by_cols)
        own, oth = (down0[...], down1[...]) if m == 2 else (gu[m * 256 : (m + 1) * 256, :] for gu in (gu0, gu1))
        total = lax.dot_general(x_own[:, cols], own, dims, preferred_element_type=F32)
        total = total + lax.dot_general(x_oth[:, cols], oth, dims, preferred_element_type=F32)
        put_tiles(parts, m, total[:PADDED], place[1])
        put_tiles(parts, m, total[PADDED:], 1 - place[1])
        here = pl.ds(m * SIZE, SIZE)
        copies.append(pltpu.make_async_copy(parts.at[:, here], out.at[:, here], sems.at[m]))
        copies[-1].start()
    for copy in copies:
        copy.wait()


def activation_kernel(parts, acts):
    total = parts[0].astype(F32)
    for i in range(1, 16):
        total = total + parts[i].astype(F32)
    gate, up, back = total[:SIZE], total[SIZE : 2 * SIZE], total[2 * SIZE :]
    logistic = jax.nn.sigmoid(gate)
    hidden = (gate * logistic * up).astype(BF16)
    grad_gate_act = (back * up * logistic * (1.0 + gate * (1.0 - logistic))).astype(BF16)
    grad_up_act = (back * gate * logistic).astype(BF16)
    for i in range(8):
        acts[i, :SIZE, :] = grad_gate_act
        acts[i, SIZE : 2 * SIZE, :] = grad_up_act
        acts[i, 2 * SIZE :, :] = hidden


HALVES = (pl.ds(0, 448), pl.ds(448, 448))


def token_grad_kernel(place, acts, gu0, gu1, t2_hbm, t3_hbm, out, gate_act, up_act, wide, ts, sems):
    copies = [
        [pltpu.make_async_copy(t_hbm.at[rows], ts.at[k, rows], sems.at[k, i]) for i, rows in enumerate(parts)]
        for k, t_hbm, parts in ((0, t2_hbm, HALVES), (1, t3_hbm, HALVES))
    ]
    for copy in copies[0] + copies[1]:
        copy.start()
    get_tiles(acts, 0, gate_act, 0)
    get_tiles(acts, 1, up_act, 0)
    contract_cols = (((1,), (1,)), ((), ()))
    for k in range(4):
        if k < 2:
            gu = (gu0, gu1)[k]
            part = lax.dot_general(gate_act[...], gu[:256, :], contract_cols, preferred_element_type=F32)
            part = part + lax.dot_general(up_act[...], gu[256:, :], contract_cols, preferred_element_type=F32)
        else:
            for copy in copies[k - 2]:
                copy.wait()
            part = jnp.dot(gate_act[...], ts[k - 2, :, :256], preferred_element_type=F32)
            part = part + jnp.dot(up_act[...], ts[k - 2, :, 256:], preferred_element_type=F32)
        for j in range(2):
            wide[k // 2, pl.ds(k % 2 * 2 + j, QUARTER, stride=4), :] = tile(part[:QUARTER], j)
    for far in range(2):
        for i in range(8):
            rows = wide[far, i * 4 * ROWS : (i + 1) * 4 * ROWS, :]
            out[lax.rem(far + place[4], 2) * 8 + came_from(place[2 + far], i)] = rows.astype(BF16)


def token_sum_kernel(place, parts, out, total):
    odd = place[0] == 1
    acc = parts[0].astype(F32)
    for t in range(1, 16):
        acc = acc + parts[t].astype(F32)
    total[...] = acc
    pieces = [total[pl.ds(j, ROWS, stride=4), :] for j in range(4)]
    for j in range(4):
        out[:, j * 128 : (j + 1) * 128] = jnp.where(odd, pieces[(j + 2) % 4], pieces[j]).astype(BF16)


def weight_grad_kernel(x_own, x_got, acts0, acts1, acts2, acts3, grad_gate, grad_up, grad_down, x, act):
    contract_rows = (((0,), (0,)), ((), ()))
    for k in range(4):
        rows = slice(k // 2 * PADDED, (k // 2 + 1) * PADDED)
        x[k * PADDED : (k + 1) * PADDED, :] = (x_got if k % 2 else x_own)[rows, :]
    for m in range(3):
        for k, acts in enumerate((acts0, acts1, acts2, acts3)):
            get_tiles(acts, m, act, k * PADDED)
        if m < 2:
            out, left, right = (grad_gate, grad_up)[m], x[:, :256], act[...]
        else:
            out, left, right = grad_down, act[...], x[:, 256:]
        out[...] = lax.dot_general(left, right, contract_rows, preferred_element_type=F32).astype(BF16)


def copy_kernel(x, out):
    out[...] = x[...]


def after(x, *deps):
    return call(copy_kernel, (shape(*x.shape, dtype=x.dtype),), (x,), deps=deps)[0]


def after_in_hbm(x, dep):
    return pl.pallas_call(
        lambda *refs: None,
        out_shape=pltpu.HBM(x.shape, x.dtype),
        in_specs=[HBM, VMEM],
        out_specs=HBM,
        input_output_aliases={0: 0},
        compiler_params=PARAMS,
    )(in_hbm(x), dep)


def in_hbm(x):
    return pltpu.with_memory_space_constraint(x, pltpu.HBM)


def swap(axis, x):
    return lax.ppermute(x, axis, [(0, 1), (1, 0)])


def place_of(z, xh, core, xl, y):
    return (((z * 2 + xh) * 2 + core) * 2 + xl) * 8 + y


def permutation(to):
    grid = [(z, xh, c, xl, y) for z in range(8) for xh in range(2) for c in range(2) for xl in range(2) for y in range(8)]
    return [(place_of(*at), place_of(*to(*at))) for at in grid]


def per_device(tokens, cotangent, gate_weight, up_weight, down_weight):
    z, xh, core = (lax.axis_index(axis) for axis in FSDP)
    base = z + 4 + z % 4 * 2
    place = jnp.stack([core, xh, (base + xh) % 8, (base + 1 - xh) % 8, z // 4]).astype(jnp.int32)
    def chip(z, xl, y):
        return 4 * xl + y // 2, (y + 4 - z + 4 * xl + y // 2) % 8

    def forth(z, xh, c, xl, y):
        to, row = chip(z, xl, y)
        return to, y % 2, c, xh ^ y % 2 ^ xl, row

    def back(z, xh, c, xl, y):
        to, row = chip(z, xl, y)
        return to, xh, c, xh ^ y % 2 ^ xl, row

    there = permutation(forth)
    home = [(b, a) for a, b in permutation(back)]

    packed, ready0 = call(
        pack_kernel,
        (shape(88, 128),),
        (place, in_hbm(tokens), in_hbm(cotangent)),
        [
            pltpu.VMEM((88, 128), F32),
            pltpu.VMEM((ROWS, 512), BF16),
            pltpu.VMEM((ROWS, 512), BF16),
            pltpu.SemaphoreType.DMA((2,)),
        ],
        specs=[SMEM, HBM, HBM],
    )
    packed = lax.ppermute(packed, ALL, there)
    spread, _ = call(spread_kernel, (shape(16, 88, 128),), (packed,), flops=10**11)
    rows = lax.all_to_all(spread, TENSOR, 0, 0, tiled=True)
    gu0, _ = call(
        weights_kernel,
        (shape(512, 896),),
        (in_hbm(gate_weight), in_hbm(up_weight)),
        [pltpu.SemaphoreType.DMA((2,))],
        specs=[HBM, HBM],
        deps=(ready0,),
    )
    gu1, down1 = swap("core", gu0), swap("core", down_weight)

    parts, x_own, x_oth, ready = call(
        forward_kernel,
        (pltpu.HBM((16, 3 * SIZE, 128), BF16), *[pltpu.HBM((2 * PADDED, 512), BF16)] * 2),
        (place, rows, gu0, gu1, down_weight, down1),
        [
            pltpu.VMEM((16 * 88, 128), F32),
            pltpu.VMEM((16, 3 * SIZE, 128), BF16),
            pltpu.VMEM((2 * PADDED, 512), BF16),
            pltpu.VMEM((2 * PADDED, 512), BF16),
            pltpu.SemaphoreType.DMA((5,)),
        ],
        specs=[SMEM] + [VMEM] * 5,
        outs=[HBM] * 3,
    )
    parts = lax.all_to_all(parts, ("z", "xh"), 0, 0, tiled=True)
    x_got = swap("core", after(x_oth, ready))
    t0, _ = call(transpose_kernel, (shape(896, 512),), (gu0,), deps=(ready,))
    t2 = swap("xh", t0)

    acts0, ready = call(activation_kernel, (shape(8, 3 * SIZE, 128),), (parts,))
    acts0 = lax.all_to_all(acts0, "z", 0, 0, tiled=True)
    t2 = after_in_hbm(t2, ready)
    t3 = swap("core", t2)
    token_parts, ready = call(
        token_grad_kernel,
        (shape(16, 4 * ROWS, 128),),
        (place, acts0, gu0, gu1, in_hbm(t2), in_hbm(t3)),
        [
            pltpu.VMEM((PADDED, 896), BF16),
            pltpu.VMEM((PADDED, 896), BF16),
            pltpu.VMEM((2, 4 * QUARTER, 128), F32),
            pltpu.VMEM((2, 896, 512), BF16),
            pltpu.SemaphoreType.DMA((2, 2)),
        ],
        specs=[SMEM] + [VMEM] * 3 + [HBM] * 2,
        deps=(x_got,),
    )
    token_parts = lax.all_to_all(token_parts, TENSOR, 0, 0, tiled=True)
    acts2 = swap("xh", acts0)
    acts1 = swap("core", acts0)
    acts3 = swap("core", acts2)

    grad_tokens, _ = call(
        token_sum_kernel,
        (shape(ROWS, 512),),
        (place, token_parts),
        [pltpu.VMEM((4 * ROWS, 128), F32)],
        specs=[SMEM, VMEM],
        flops=10**11,
    )
    grad_tokens = lax.ppermute(grad_tokens, ALL, home)

    grad_gate, grad_up, grad_down, ready = call(
        weight_grad_kernel,
        (shape(256, 896), shape(256, 896), shape(896, 256)),
        (x_own, x_got, acts0, acts1, acts2, acts3),
        [pltpu.VMEM((4 * PADDED, 512), BF16), pltpu.VMEM((4 * PADDED, 896), BF16)],
    )
    return (after(grad_tokens, ready), grad_gate, grad_up, grad_down)


def solution(mesh):
    chips = Mesh(mesh.devices.reshape(8, 2, 2, 2, 8), ALL)
    rows, cols = P(FSDP, TENSOR), P(TENSOR, FSDP)
    return jax.shard_map(
        per_device,
        mesh=chips,
        in_specs=(rows, rows, rows, rows, cols),
        out_specs=(rows, rows, rows, cols),
        check_vma=False,
    )
```

```python
import math

import jax
import jax.numpy as jnp
from jax import lax
from jax.experimental import pallas as pl
from jax.experimental.pallas import tpu as pltpu
from jax.sharding import Mesh
from jax.sharding import PartitionSpec as P

F32, BF16 = jnp.float32, jnp.bfloat16
ALL = ("z", "xh", "core", "xl", "y")
FSDP = ("z", "xh", "core")
TENSOR = ("xl", "y")
AROUND = ("y", "xl")

ROWS, QUARTER, PADDED = 11, 88, 96
UP, ACROSS, PER = 5, 7, 5
SIZE = PER * 16
VMEM = pl.BlockSpec(memory_space=pltpu.VMEM)
HBM = pl.BlockSpec(memory_space=pltpu.HBM)
SMEM = pl.BlockSpec(memory_space=pltpu.SMEM)
PARAMS = pltpu.CompilerParams(vmem_limit_bytes=20 * 1024 * 1024)


def call(kernel, out_shape, inputs, scratch=(), specs=None, flops=0, deps=(), outs=None):
    moved = sum(x.size * x.dtype.itemsize for x in inputs)
    moved += sum(math.prod(s.shape) * s.dtype.itemsize for s in out_shape)
    n, m = len(inputs), len(out_shape)

    def body(*refs):
        rest = refs[n + len(deps) :]
        rest[m][...] = jnp.zeros((8, 128), F32)
        kernel(*refs[:n], *rest[:m], *rest[m + 1 :])

    return pl.pallas_call(
        body,
        out_shape=(*out_shape, shape(8, 128, dtype=F32)),
        in_specs=list(specs or [VMEM] * n) + [VMEM] * len(deps),
        out_specs=list(outs or [VMEM] * m) + [VMEM],
        scratch_shapes=list(scratch),
        compiler_params=PARAMS,
        cost_estimate=pl.CostEstimate(flops=flops, bytes_accessed=moved, transcendentals=0),
    )(*inputs, *deps)


def shape(*dims, dtype=BF16):
    return jax.ShapeDtypeStruct(dims, dtype)


def tile(ref_or_value, j):
    return ref_or_value[:, j * 128 : (j + 1) * 128]


def fetch(sems, *pairs):
    copies = [pltpu.make_async_copy(source, to, sems.at[i]) for i, (source, to) in enumerate(pairs)]
    for copy in copies:
        copy.start()
    for copy in copies:
        copy.wait()


def pack_kernel(place, tok_hbm, cot_hbm, out, wide, tok, cot, sems):
    fetch(sems, (tok_hbm, tok), (cot_hbm, cot))
    odd = place[0] == 1
    for base, ref in ((0, tok), (4, cot)):
        rows = ref[...].astype(F32)
        for j in range(4):
            piece = jnp.where(odd, tile(rows, (j + 2) % 4), tile(rows, j))
            wide[pl.ds(base + j, ROWS, stride=8), :] = piece
    out[...] = wide[...].astype(BF16)


def put_tiles(out, m, value, half):
    def put(slot, rows):
        row = m * SIZE + slot % PER * 16
        out[half * 8 + slot // PER, row : row + 16, :] = rows.astype(BF16)

    blank = jnp.zeros((8, 128), F32)
    for i in range(UP):
        for j in range(ACROSS):
            put(i * ACROSS + j, tile(value[i * 16 : (i + 1) * 16], j))
    last = [tile(value[UP * 16 : QUARTER], j) for j in range(ACROSS)] + [blank] * 3
    for j in range(0, 10, 2):
        put(UP * ACROSS + j // 2, jnp.concatenate([last[j], last[j + 1]], axis=0))


def get_tiles(ref, m, out, first):
    def get(slot):
        row = m * SIZE + slot % PER * 16
        return ref[slot // PER, row : row + 16, :]

    blank = jnp.zeros((8, 128), F32)
    for i in range(UP):
        for j in range(ACROSS):
            out[first + i * 16 : first + (i + 1) * 16, j * 128 : (j + 1) * 128] = get(i * ACROSS + j)
    for j in range(ACROSS):
        pair = get(UP * ACROSS + j // 2).astype(F32)
        half = pair[8:] if j % 2 else pair[:8]
        rows = jnp.concatenate([half, blank], axis=0).astype(BF16)
        out[first + UP * 16 : first + PADDED, j * 128 : (j + 1) * 128] = rows


def weights_kernel(gate_weight, up_weight, out, sems):
    fetch(sems, (gate_weight, out.at[:256]), (up_weight, out.at[256:]))


def spread_kernel(packed, out):
    for t in range(16):
        out[t] = packed[...]


def came_from(base, i):
    return lax.rem(base - i + 8, 8)


def transpose_kernel(gu, out):
    out[:, :256] = gu[:256, :].T
    out[:, 256:] = gu[256:, :].T


def forward_kernel(
    place, rows, gu0, gu1, down0, down1, out, own_out, oth_out, wide, parts, x_own, x_oth, sems
):
    for far in range(2):
        for i in range(8):
            at = (far * 8 + i) * 88
            wide[at : at + 88, :] = rows[came_from(place[2], i) * 2 + lax.rem(far + place[4], 2)].astype(F32)
    blank = jnp.zeros((PADDED - QUARTER, 128), F32)
    for far in range(2):
        for j in range(8):
            piece = jnp.concatenate([wide[pl.ds(far * 704 + j, QUARTER, stride=8), :], blank], axis=0)
            at = (j // 4 * 2 + j % 2) * 128
            ref = (x_own, x_oth)[j % 4 // 2]
            ref[far * PADDED : (far + 1) * PADDED, at : at + 128] = piece.astype(BF16)
    by_cols = (((1,), (0,)), ((), ()))
    by_rows = (((1,), (1,)), ((), ()))
    copies = [
        pltpu.make_async_copy(x_own, own_out, sems.at[3]),
        pltpu.make_async_copy(x_oth, oth_out, sems.at[4]),
    ]
    for copy in copies:
        copy.start()
    for m in range(3):
        cols, dims = (slice(256, 512), by_rows) if m == 2 else (slice(0, 256), by_cols)
        own, oth = (down0[...], down1[...]) if m == 2 else (gu[m * 256 : (m + 1) * 256, :] for gu in (gu0, gu1))
        total = lax.dot_general(x_own[:, cols], own, dims, preferred_element_type=F32)
        total = total + lax.dot_general(x_oth[:, cols], oth, dims, preferred_element_type=F32)
        put_tiles(parts, m, total[:PADDED], place[1])
        put_tiles(parts, m, total[PADDED:], 1 - place[1])
        here = pl.ds(m * SIZE, SIZE)
        copies.append(pltpu.make_async_copy(parts.at[:, here], out.at[:, here], sems.at[m]))
        copies[-1].start()
    for copy in copies:
        copy.wait()


def activation_kernel(parts, acts):
    total = parts[0].astype(F32)
    for i in range(1, 16):
        total = total + parts[i].astype(F32)
    gate, up, back = total[:SIZE], total[SIZE : 2 * SIZE], total[2 * SIZE :]
    logistic = jax.nn.sigmoid(gate)
    hidden = (gate * logistic * up).astype(BF16)
    grad_gate_act = (back * up * logistic * (1.0 + gate * (1.0 - logistic))).astype(BF16)
    grad_up_act = (back * gate * logistic).astype(BF16)
    for i in range(8):
        acts[i, :SIZE, :] = grad_gate_act
        acts[i, SIZE : 2 * SIZE, :] = grad_up_act
        acts[i, 2 * SIZE :, :] = hidden


HALVES = (pl.ds(0, 448), pl.ds(448, 448))


def token_grad_kernel(place, acts, gu0, gu1, t2_hbm, t3_hbm, out, gate_act, up_act, wide, ts, sems):
    copies = [
        [pltpu.make_async_copy(t_hbm.at[rows], ts.at[k, rows], sems.at[k, i]) for i, rows in enumerate(parts)]
        for k, t_hbm, parts in ((0, t2_hbm, HALVES), (1, t3_hbm, HALVES))
    ]
    for copy in copies[0] + copies[1]:
        copy.start()
    get_tiles(acts, 0, gate_act, 0)
    get_tiles(acts, 1, up_act, 0)
    contract_cols = (((1,), (1,)), ((), ()))
    for k in range(4):
        if k < 2:
            gu = (gu0, gu1)[k]
            part = lax.dot_general(gate_act[...], gu[:256, :], contract_cols, preferred_element_type=F32)
            part = part + lax.dot_general(up_act[...], gu[256:, :], contract_cols, preferred_element_type=F32)
        else:
            for copy in copies[k - 2]:
                copy.wait()
            part = jnp.dot(gate_act[...], ts[k - 2, :, :256], preferred_element_type=F32)
            part = part + jnp.dot(up_act[...], ts[k - 2, :, 256:], preferred_element_type=F32)
        for j in range(2):
            wide[k // 2, pl.ds(k % 2 * 2 + j, QUARTER, stride=4), :] = tile(part[:QUARTER], j)
    for far in range(2):
        for i in range(8):
            rows = wide[far, i * 4 * ROWS : (i + 1) * 4 * ROWS, :]
            out[came_from(place[2 + far], i) * 2 + lax.rem(far + place[4], 2)] = rows.astype(BF16)


def token_sum_kernel(place, parts, out, total):
    odd = place[0] == 1
    acc = parts[0].astype(F32)
    for t in range(1, 16):
        acc = acc + parts[t].astype(F32)
    total[...] = acc
    pieces = [total[pl.ds(j, ROWS, stride=4), :] for j in range(4)]
    for j in range(4):
        out[:, j * 128 : (j + 1) * 128] = jnp.where(odd, pieces[(j + 2) % 4], pieces[j]).astype(BF16)


def weight_grad_kernel(x_own, x_got, acts0, acts1, acts2, acts3, grad_gate, grad_up, grad_down, x, act):
    contract_rows = (((0,), (0,)), ((), ()))
    for k in range(4):
        rows = slice(k // 2 * PADDED, (k // 2 + 1) * PADDED)
        x[k * PADDED : (k + 1) * PADDED, :] = (x_got if k % 2 else x_own)[rows, :]
    for m in range(3):
        for k, acts in enumerate((acts0, acts1, acts2, acts3)):
            get_tiles(acts, m, act, k * PADDED)
        if m < 2:
            out, left, right = (grad_gate, grad_up)[m], x[:, :256], act[...]
        else:
            out, left, right = grad_down, act[...], x[:, 256:]
        out[...] = lax.dot_general(left, right, contract_rows, preferred_element_type=F32).astype(BF16)


def copy_kernel(x, out):
    out[...] = x[...]


def after(x, *deps):
    return call(copy_kernel, (shape(*x.shape, dtype=x.dtype),), (x,), deps=deps)[0]


def after_in_hbm(x, *deps):
    return pl.pallas_call(
        lambda *refs: None,
        out_shape=pltpu.HBM(x.shape, x.dtype),
        in_specs=[HBM] + [VMEM] * len(deps),
        out_specs=HBM,
        input_output_aliases={0: 0},
        compiler_params=PARAMS,
    )(in_hbm(x), *deps)


def in_hbm(x):
    return pltpu.with_memory_space_constraint(x, pltpu.HBM)


def swap(axis, x):
    return lax.ppermute(x, axis, [(0, 1), (1, 0)])


def place_of(z, xh, core, xl, y):
    return (((z * 2 + xh) * 2 + core) * 2 + xl) * 8 + y


def permutation(to):
    grid = [(z, xh, c, xl, y) for z in range(8) for xh in range(2) for c in range(2) for xl in range(2) for y in range(8)]
    return [(place_of(*at), place_of(*to(*at))) for at in grid]


def per_device(tokens, cotangent, gate_weight, up_weight, down_weight):
    z, xh, core = (lax.axis_index(axis) for axis in FSDP)
    base = z + 4 + z % 4 * 2
    place = jnp.stack([core, xh, (base + xh) % 8, (base + 1 - xh) % 8, z // 4]).astype(jnp.int32)
    def chip(z, xl, y):
        return 4 * xl + y // 2, (y + 4 - z + 4 * xl + y // 2) % 8

    def forth(z, xh, c, xl, y):
        to, row = chip(z, xl, y)
        return to, y % 2, c, xh ^ y % 2 ^ xl, row

    def back(z, xh, c, xl, y):
        to, row = chip(z, xl, y)
        return to, xh, c, xh ^ y % 2 ^ xl, row

    there = permutation(forth)
    home = [(b, a) for a, b in permutation(back)]

    packed, ready0 = call(
        pack_kernel,
        (shape(88, 128),),
        (place, in_hbm(tokens), in_hbm(cotangent)),
        [
            pltpu.VMEM((88, 128), F32),
            pltpu.VMEM((ROWS, 512), BF16),
            pltpu.VMEM((ROWS, 512), BF16),
            pltpu.SemaphoreType.DMA((2,)),
        ],
        specs=[SMEM, HBM, HBM],
    )
    packed = lax.ppermute(packed, ALL, there)
    spread, _ = call(spread_kernel, (shape(16, 88, 128),), (packed,), flops=10**11)
    rows = lax.all_to_all(spread, AROUND, 0, 0, tiled=True)
    gu0, _ = call(
        weights_kernel,
        (shape(512, 896),),
        (in_hbm(gate_weight), in_hbm(up_weight)),
        [pltpu.SemaphoreType.DMA((2,))],
        specs=[HBM, HBM],
        deps=(ready0,),
    )
    gu1, down1 = swap("core", gu0), swap("core", down_weight)

    parts, x_own, x_oth, ready = call(
        forward_kernel,
        (pltpu.HBM((16, 3 * SIZE, 128), BF16), *[pltpu.HBM((2 * PADDED, 512), BF16)] * 2),
        (place, rows, gu0, gu1, down_weight, down1),
        [
            pltpu.VMEM((16 * 88, 128), F32),
            pltpu.VMEM((16, 3 * SIZE, 128), BF16),
            pltpu.VMEM((2 * PADDED, 512), BF16),
            pltpu.VMEM((2 * PADDED, 512), BF16),
            pltpu.SemaphoreType.DMA((5,)),
        ],
        specs=[SMEM] + [VMEM] * 5,
        outs=[HBM] * 3,
    )
    parts = lax.all_to_all(parts, ("xh", "z"), 0, 0, tiled=True)
    x_got = swap("core", after(x_oth, ready))
    t0, _ = call(transpose_kernel, (shape(896, 512),), (gu0,), deps=(ready,))
    t2 = swap("xh", t0)

    acts0, ready = call(activation_kernel, (shape(8, 3 * SIZE, 128),), (parts,))
    acts0 = lax.all_to_all(acts0, "z", 0, 0, tiled=True)
    t2 = after_in_hbm(t2, ready, x_got)
    t3 = swap("core", t2)
    token_parts, ready = call(
        token_grad_kernel,
        (shape(16, 4 * ROWS, 128),),
        (place, acts0, gu0, gu1, in_hbm(t2), in_hbm(t3)),
        [
            pltpu.VMEM((PADDED, 896), BF16),
            pltpu.VMEM((PADDED, 896), BF16),
            pltpu.VMEM((2, 4 * QUARTER, 128), F32),
            pltpu.VMEM((2, 896, 512), BF16),
            pltpu.SemaphoreType.DMA((2, 2)),
        ],
        specs=[SMEM] + [VMEM] * 3 + [HBM] * 2,
    )
    token_parts = lax.all_to_all(token_parts, AROUND, 0, 0, tiled=True)
    acts2 = swap("xh", acts0)
    acts1 = swap("core", acts0)
    acts3 = swap("core", acts2)

    grad_tokens, _ = call(
        token_sum_kernel,
        (shape(ROWS, 512),),
        (place, token_parts),
        [pltpu.VMEM((4 * ROWS, 128), F32)],
        specs=[SMEM, VMEM],
        flops=10**11,
    )
    grad_tokens = lax.ppermute(grad_tokens, ALL, home)

    grad_gate, grad_up, grad_down, ready = call(
        weight_grad_kernel,
        (shape(256, 896), shape(256, 896), shape(896, 256)),
        (x_own, x_got, acts0, acts1, acts2, acts3),
        [pltpu.VMEM((4 * PADDED, 512), BF16), pltpu.VMEM((4 * PADDED, 896), BF16)],
    )
    return (after(grad_tokens, ready), grad_gate, grad_up, grad_down)


def solution(mesh):
    chips = Mesh(mesh.devices.reshape(8, 2, 2, 2, 8), ALL)
    rows, cols = P(FSDP, TENSOR), P(TENSOR, FSDP)
    return jax.shard_map(
        per_device,
        mesh=chips,
        in_specs=(rows, rows, rows, rows, cols),
        out_specs=(rows, rows, rows, cols),
        check_vma=False,
    )
```

```python
import math

import jax
import jax.numpy as jnp
from jax import lax
from jax.experimental import pallas as pl
from jax.experimental.pallas import tpu as pltpu
from jax.sharding import Mesh
from jax.sharding import PartitionSpec as P

F32, BF16 = jnp.float32, jnp.bfloat16
ALL = ("z", "xh", "core", "xl", "y")
FSDP = ("z", "xh", "core")
TENSOR = ("xl", "y")
AROUND = ("y", "xl")

ROWS, QUARTER, PADDED = 11, 88, 96
BLOCK = 48
UP, ACROSS, PER = 5, 7, 5
SIZE = PER * 16
VMEM = pl.BlockSpec(memory_space=pltpu.VMEM)
HBM = pl.BlockSpec(memory_space=pltpu.HBM)
PARAMS = pltpu.CompilerParams(vmem_limit_bytes=20 * 1024 * 1024)


def call(kernel, out_shape, inputs, scratch=(), specs=None, flops=0, deps=(), outs=None, token=True):
    moved = sum(x.size * x.dtype.itemsize for x in inputs)
    moved += sum(math.prod(s.shape) * s.dtype.itemsize for s in out_shape)
    n, m = len(inputs), len(out_shape)

    def body(*refs):
        rest = refs[n + len(deps) :]
        if token:
            rest[m][...] = jnp.zeros((8, 128), F32)
        kernel(*refs[:n], *rest[:m], *rest[m + token :])

    return pl.pallas_call(
        body,
        out_shape=(*out_shape, *[shape(8, 128, dtype=F32)] * token),
        in_specs=list(specs or [VMEM] * n) + [VMEM] * len(deps),
        out_specs=list(outs or [VMEM] * m) + [VMEM] * token,
        scratch_shapes=list(scratch),
        compiler_params=PARAMS,
        cost_estimate=pl.CostEstimate(flops=flops, bytes_accessed=moved, transcendentals=0),
    )(*inputs, *deps)


def shape(*dims, dtype=BF16):
    return jax.ShapeDtypeStruct(dims, dtype)


def tile(ref_or_value, j):
    return ref_or_value[:, j * 128 : (j + 1) * 128]


def fetch(sems, *pairs):
    copies = [pltpu.make_async_copy(source, to, sems.at[i]) for i, (source, to) in enumerate(pairs)]
    for copy in copies:
        copy.start()
    for copy in copies:
        copy.wait()


def here():
    z, xh, core = (lax.axis_index(axis) for axis in FSDP)
    base = z + 4 + lax.rem(z, 4) * 2
    return core, xh, lax.rem(base + xh, 8), lax.rem(base + 1 - xh, 8), z // 4


def pack_kernel(tok_hbm, cot_hbm, out, wide, tok, cot, sems):
    fetch(sems, (tok_hbm, tok), (cot_hbm, cot))
    odd = here()[0] == 1
    for base, ref in ((0, tok), (4, cot)):
        rows = ref[...].astype(F32)
        for j in range(4):
            piece = jnp.where(odd, tile(rows, (j + 2) % 4), tile(rows, j))
            wide[pl.ds(base + j, ROWS, stride=8), :] = piece
    out[...] = wide[:88, :].astype(BF16)


def put_tiles(out, m, value, half):
    def put(slot, rows):
        row = m * SIZE + slot % PER * 16
        out[half * 8 + slot // PER, row : row + 16, :] = rows.astype(BF16)

    blank = jnp.zeros((8, 128), F32)
    for i in range(UP):
        for j in range(ACROSS):
            put(i * ACROSS + j, tile(value[i * 16 : (i + 1) * 16], j))
    last = [tile(value[UP * 16 : QUARTER], j) for j in range(ACROSS)] + [blank] * 3
    for j in range(0, 10, 2):
        put(UP * ACROSS + j // 2, jnp.concatenate([last[j], last[j + 1]], axis=0))


def get_tiles(ref, m, out, first):
    def get(slot):
        row = m * SIZE + slot % PER * 16
        return ref[slot // PER, row : row + 16, :]

    blank = jnp.zeros((8, 128), F32)
    for i in range(UP):
        for j in range(ACROSS):
            out[first + i * 16 : first + (i + 1) * 16, j * 128 : (j + 1) * 128] = get(i * ACROSS + j)
    for j in range(ACROSS):
        pair = get(UP * ACROSS + j // 2).astype(F32)
        half = pair[8:] if j % 2 else pair[:8]
        rows = jnp.concatenate([half, blank], axis=0).astype(BF16)
        out[first + UP * 16 : first + PADDED, j * 128 : (j + 1) * 128] = rows


def weights_kernel(gate_weight, up_weight, out, sems):
    fetch(sems, (gate_weight, out.at[:256]), (up_weight, out.at[256:]))


def spread_kernel(packed, out):
    for t in range(16):
        out[t] = packed[...]


def came_from(base, i):
    return lax.rem(base - i + 8, 8)


def transpose_kernel(gu, out):
    out[:, :256] = gu[:256, :].T
    out[:, 256:] = gu[256:, :].T


def forward_kernel(
    rows, gu0, gu1, down0, down1, out, own_out, oth_out, wide, parts, x_own, x_oth, sems
):
    place = here()
    for far in range(2):
        for i in range(8):
            at = (far * 8 + i) * 88
            wide[at : at + 88, :] = rows[came_from(place[2], i) * 2 + lax.rem(far + place[4], 2)].astype(F32)
    blank = jnp.zeros((PADDED - QUARTER, 128), F32)
    for far in range(2):
        for j in range(8):
            piece = jnp.concatenate([wide[pl.ds(far * 704 + j, QUARTER, stride=8), :], blank], axis=0)
            at = (j // 4 * 2 + j % 2) * 128
            ref = (x_own, x_oth)[j % 4 // 2]
            ref[far * PADDED : (far + 1) * PADDED, at : at + 128] = piece.astype(BF16)
    by_cols = (((1,), (0,)), ((), ()))
    by_rows = (((1,), (1,)), ((), ()))
    copies = [
        pltpu.make_async_copy(x_own, own_out, sems.at[3]),
        pltpu.make_async_copy(x_oth, oth_out, sems.at[4]),
    ]
    for copy in copies:
        copy.start()
    for m in range(3):
        cols, dims = (slice(256, 512), by_rows) if m == 2 else (slice(0, 256), by_cols)
        own, oth = (down0[...], down1[...]) if m == 2 else (gu[m * 256 : (m + 1) * 256, :] for gu in (gu0, gu1))
        total = lax.dot_general(x_own[:, cols], own, dims, preferred_element_type=F32)
        total = total + lax.dot_general(x_oth[:, cols], oth, dims, preferred_element_type=F32)
        put_tiles(parts, m, total[:PADDED], place[1])
        put_tiles(parts, m, total[PADDED:], 1 - place[1])
        which = pl.ds(m * SIZE, SIZE)
        copies.append(pltpu.make_async_copy(parts.at[:, which], out.at[:, which], sems.at[m]))
        copies[-1].start()
    for copy in copies:
        copy.wait()


def activation_kernel(parts, acts):
    total = parts[0].astype(F32)
    for i in range(1, 16):
        total = total + parts[i].astype(F32)
    gate, up, back = total[:SIZE], total[SIZE : 2 * SIZE], total[2 * SIZE :]
    logistic = jax.nn.sigmoid(gate)
    hidden = (gate * logistic * up).astype(BF16)
    grad_gate_act = (back * up * logistic * (1.0 + gate * (1.0 - logistic))).astype(BF16)
    grad_up_act = (back * gate * logistic).astype(BF16)
    for i in range(8):
        acts[i, :SIZE, :] = grad_gate_act
        acts[i, SIZE : 2 * SIZE, :] = grad_up_act
        acts[i, 2 * SIZE :, :] = hidden


HALVES = (pl.ds(0, 448), pl.ds(448, 448))


def token_grad_kernel(acts, gu0, gu1, t2_hbm, t3_hbm, out, gate_act, up_act, wide, ts, sems):
    copies = [
        [pltpu.make_async_copy(t_hbm.at[rows], ts.at[k, rows], sems.at[k, i]) for i, rows in enumerate(parts)]
        for k, t_hbm, parts in ((0, t2_hbm, HALVES), (1, t3_hbm, HALVES))
    ]
    for copy in copies[0] + copies[1]:
        copy.start()
    get_tiles(acts, 0, gate_act, 0)
    get_tiles(acts, 1, up_act, 0)
    place = here()
    contract_cols = (((1,), (1,)), ((), ()))
    for k in range(4):
        if k < 2:
            gu = (gu0, gu1)[k]
            part = lax.dot_general(gate_act[...], gu[:256, :], contract_cols, preferred_element_type=F32)
            part = part + lax.dot_general(up_act[...], gu[256:, :], contract_cols, preferred_element_type=F32)
        else:
            for copy in copies[k - 2]:
                copy.wait()
            part = jnp.dot(gate_act[...], ts[k - 2, :, :256], preferred_element_type=F32)
            part = part + jnp.dot(up_act[...], ts[k - 2, :, 256:], preferred_element_type=F32)
        for j in range(2):
            wide[k // 2, pl.ds(k % 2 * 2 + j, QUARTER, stride=4), :] = tile(part[:QUARTER], j)
    wide[:, 4 * QUARTER :, :] = jnp.zeros((2, 8, 128), F32)
    for far in range(2):
        for i in range(8):
            rows = wide[far, i * 4 * ROWS : i * 4 * ROWS + BLOCK, :]
            out[came_from(place[2 + far], i) * 2 + lax.rem(far + place[4], 2)] = rows.astype(BF16)


def token_sum_kernel(parts, out, total):
    odd = here()[0] == 1
    acc = parts[0].astype(F32)
    for t in range(1, 16):
        acc = acc + parts[t].astype(F32)
    total[...] = acc
    pieces = [total[pl.ds(j, ROWS, stride=4), :] for j in range(4)]
    for j in range(4):
        out[:, j * 128 : (j + 1) * 128] = jnp.where(odd, pieces[(j + 2) % 4], pieces[j]).astype(BF16)


def weight_grad_kernel(x_own, x_got, acts0, acts1, acts2, acts3, grad_gate, grad_up, grad_down, x, act):
    contract_rows = (((0,), (0,)), ((), ()))
    for k in range(4):
        rows = slice(k // 2 * PADDED, (k // 2 + 1) * PADDED)
        x[k * PADDED : (k + 1) * PADDED, :] = (x_got if k % 2 else x_own)[rows, :]
    for m in range(3):
        for k, acts in enumerate((acts0, acts1, acts2, acts3)):
            get_tiles(acts, m, act, k * PADDED)
        if m < 2:
            out, left, right = (grad_gate, grad_up)[m], x[:, :256], act[...]
        else:
            out, left, right = grad_down, act[...], x[:, 256:]
        out[...] = lax.dot_general(left, right, contract_rows, preferred_element_type=F32).astype(BF16)


def copy_kernel(x, out):
    out[...] = x[...]


def after(x, *deps):
    return call(copy_kernel, (shape(*x.shape, dtype=x.dtype),), (x,), deps=deps, token=False)[0]


def after_in_hbm(x, *deps):
    return pl.pallas_call(
        lambda *refs: None,
        out_shape=pltpu.HBM(x.shape, x.dtype),
        in_specs=[HBM] + [VMEM] * len(deps),
        out_specs=HBM,
        input_output_aliases={0: 0},
        compiler_params=PARAMS,
    )(in_hbm(x), *deps)


def in_hbm(x):
    return pltpu.with_memory_space_constraint(x, pltpu.HBM)


def swap(axis, x):
    return lax.ppermute(x, axis, [(0, 1), (1, 0)])


def place_of(z, xh, core, xl, y):
    return (((z * 2 + xh) * 2 + core) * 2 + xl) * 8 + y


def permutation(to):
    grid = [(z, xh, c, xl, y) for z in range(8) for xh in range(2) for c in range(2) for xl in range(2) for y in range(8)]
    return [(place_of(*at), place_of(*to(*at))) for at in grid]


def per_device(tokens, cotangent, gate_weight, up_weight, down_weight):
    def chip(z, xl, y):
        return 4 * xl + y // 2, (y + 4 - z + 4 * xl + y // 2) % 8

    def forth(z, xh, c, xl, y):
        to, row = chip(z, xl, y)
        return to, y % 2, c, xh ^ y % 2 ^ xl, row

    def back(z, xh, c, xl, y):
        to, row = chip(z, xl, y)
        return to, xh, c, xh ^ y % 2 ^ xl, row

    there = permutation(forth)
    home = [(b, a) for a, b in permutation(back)]

    packed, ready0 = call(
        pack_kernel,
        (shape(88, 128),),
        (in_hbm(tokens), in_hbm(cotangent)),
        [
            pltpu.VMEM((96, 128), F32),
            pltpu.VMEM((ROWS, 512), BF16),
            pltpu.VMEM((ROWS, 512), BF16),
            pltpu.SemaphoreType.DMA((2,)),
        ],
        specs=[HBM, HBM],
    )
    packed = lax.ppermute(packed, ALL, there)
    (spread,) = call(spread_kernel, (shape(16, 88, 128),), (packed,), flops=10**11, token=False)
    rows = lax.all_to_all(spread, AROUND, 0, 0, tiled=True)
    (gu0,) = call(
        weights_kernel,
        (shape(512, 896),),
        (in_hbm(gate_weight), in_hbm(up_weight)),
        [pltpu.SemaphoreType.DMA((2,))],
        specs=[HBM, HBM],
        deps=(ready0,),
        token=False,
    )
    gu1, down1 = swap("core", gu0), swap("core", down_weight)

    parts, x_own, x_oth, ready = call(
        forward_kernel,
        (pltpu.HBM((16, 3 * SIZE, 128), BF16), *[pltpu.HBM((2 * PADDED, 512), BF16)] * 2),
        (rows, gu0, gu1, down_weight, down1),
        [
            pltpu.VMEM((17 * 88, 128), F32),
            pltpu.VMEM((16, 3 * SIZE, 128), BF16),
            pltpu.VMEM((2 * PADDED, 512), BF16),
            pltpu.VMEM((2 * PADDED, 512), BF16),
            pltpu.SemaphoreType.DMA((5,)),
        ],
        outs=[HBM] * 3,
    )
    parts = lax.all_to_all(parts, ("xh", "z"), 0, 0, tiled=True)
    x_got = swap("core", after(x_oth, ready))
    (t0,) = call(transpose_kernel, (shape(896, 512),), (gu0,), deps=(ready,), token=False)
    t2 = swap("xh", t0)

    acts0, ready = call(activation_kernel, (shape(8, 3 * SIZE, 128),), (parts,))
    acts0 = lax.all_to_all(acts0, "z", 0, 0, tiled=True)
    t2 = after_in_hbm(t2, ready, x_got)
    t3 = swap("core", t2)
    (token_parts,) = call(
        token_grad_kernel,
        (shape(16, BLOCK, 128),),
        (acts0, gu0, gu1, in_hbm(t2), in_hbm(t3)),
        [
            pltpu.VMEM((PADDED, 896), BF16),
            pltpu.VMEM((PADDED, 896), BF16),
            pltpu.VMEM((2, 4 * QUARTER + 8, 128), F32),
            pltpu.VMEM((2, 896, 512), BF16),
            pltpu.SemaphoreType.DMA((2, 2)),
        ],
        specs=[VMEM] * 3 + [HBM] * 2,
        token=False,
    )
    token_parts = lax.all_to_all(token_parts, AROUND, 0, 0, tiled=True)
    acts2 = swap("xh", acts0)
    acts1 = swap("core", acts0)
    acts3 = swap("core", acts2)

    (grad_tokens,) = call(
        token_sum_kernel,
        (shape(ROWS, 512),),
        (token_parts,),
        [pltpu.VMEM((BLOCK, 128), F32)],
        flops=10**11,
        token=False,
    )
    grad_tokens = lax.ppermute(grad_tokens, ALL, home)

    grad_gate, grad_up, grad_down, ready = call(
        weight_grad_kernel,
        (shape(256, 896), shape(256, 896), shape(896, 256)),
        (x_own, x_got, acts0, acts1, acts2, acts3),
        [pltpu.VMEM((4 * PADDED, 512), BF16), pltpu.VMEM((4 * PADDED, 896), BF16)],
    )
    return (after(grad_tokens, ready), grad_gate, grad_up, grad_down)


def solution(mesh):
    chips = Mesh(mesh.devices.reshape(8, 2, 2, 2, 8), ALL)
    rows, cols = P(FSDP, TENSOR), P(TENSOR, FSDP)
    return jax.shard_map(
        per_device,
        mesh=chips,
        in_specs=(rows, rows, rows, rows, cols),
        out_specs=(rows, rows, rows, cols),
        check_vma=False,
    )
```

```python
import math

import jax
import jax.numpy as jnp
from jax import lax
from jax.experimental import pallas as pl
from jax.experimental.pallas import tpu as pltpu
from jax.sharding import Mesh
from jax.sharding import PartitionSpec as P

F32, BF16 = jnp.float32, jnp.bfloat16
ALL = ("z", "xh", "core", "xl", "y")
FSDP = ("z", "xh", "core")
TENSOR = ("xl", "y")
AROUND = ("y", "xl")

ROWS, QUARTER, PADDED = 11, 88, 96
BLOCK = 48
UP, ACROSS, PER = 5, 7, 5
SIZE = PER * 16
VMEM = pl.BlockSpec(memory_space=pltpu.VMEM)
HBM = pl.BlockSpec(memory_space=pltpu.HBM)
PARAMS = pltpu.CompilerParams(vmem_limit_bytes=20 * 1024 * 1024)


def call(kernel, out_shape, inputs, scratch=(), specs=None, flops=0, deps=(), outs=None, token=True):
    moved = sum(x.size * x.dtype.itemsize for x in inputs)
    moved += sum(math.prod(s.shape) * s.dtype.itemsize for s in out_shape)
    n, m = len(inputs), len(out_shape)

    def body(*refs):
        rest = refs[n + len(deps) :]
        if token:
            rest[m][...] = jnp.zeros((8, 128), F32)
        kernel(*refs[:n], *rest[:m], *rest[m + token :])

    return pl.pallas_call(
        body,
        out_shape=(*out_shape, *[shape(8, 128, dtype=F32)] * token),
        in_specs=list(specs or [VMEM] * n) + [VMEM] * len(deps),
        out_specs=list(outs or [VMEM] * m) + [VMEM] * token,
        scratch_shapes=list(scratch),
        compiler_params=PARAMS,
        cost_estimate=pl.CostEstimate(flops=flops, bytes_accessed=moved, transcendentals=0),
    )(*inputs, *deps)


def shape(*dims, dtype=BF16):
    return jax.ShapeDtypeStruct(dims, dtype)


def tile(ref_or_value, j):
    return ref_or_value[:, j * 128 : (j + 1) * 128]


def fetch(sems, *pairs):
    copies = [pltpu.make_async_copy(source, to, sems.at[i]) for i, (source, to) in enumerate(pairs)]
    for copy in copies:
        copy.start()
    for copy in copies:
        copy.wait()


def here():
    z, xh, core = (lax.axis_index(axis) for axis in FSDP)
    base = z + 4 + lax.rem(z, 4) * 2
    return core, xh, lax.rem(base + xh, 8), lax.rem(base + 1 - xh, 8), z // 4


def pack_kernel(tok, cot, out, wide):
    odd = here()[0] == 1
    for base, ref in ((0, tok), (4, cot)):
        rows = ref[...].astype(F32)
        for j in range(4):
            piece = jnp.where(odd, tile(rows, (j + 2) % 4), tile(rows, j))
            wide[pl.ds(base + j, ROWS, stride=8), :] = piece
    out[...] = wide[:88, :].astype(BF16)


def put_tiles(out, m, value, half):
    def put(slot, rows):
        row = m * SIZE + slot % PER * 16
        out[half * 8 + slot // PER, row : row + 16, :] = rows.astype(BF16)

    blank = jnp.zeros((8, 128), F32)
    for i in range(UP):
        for j in range(ACROSS):
            put(i * ACROSS + j, tile(value[i * 16 : (i + 1) * 16], j))
    last = [tile(value[UP * 16 : QUARTER], j) for j in range(ACROSS)] + [blank] * 3
    for j in range(0, 10, 2):
        put(UP * ACROSS + j // 2, jnp.concatenate([last[j], last[j + 1]], axis=0))


def get_tiles(ref, m, out, first):
    def get(slot):
        row = m * SIZE + slot % PER * 16
        return ref[slot // PER, row : row + 16, :]

    blank = jnp.zeros((8, 128), F32)
    for i in range(UP):
        for j in range(ACROSS):
            out[first + i * 16 : first + (i + 1) * 16, j * 128 : (j + 1) * 128] = get(i * ACROSS + j)
    for j in range(ACROSS):
        pair = get(UP * ACROSS + j // 2).astype(F32)
        half = pair[8:] if j % 2 else pair[:8]
        rows = jnp.concatenate([half, blank], axis=0).astype(BF16)
        out[first + UP * 16 : first + PADDED, j * 128 : (j + 1) * 128] = rows


def weights_kernel(gate_weight, up_weight, out, sems):
    fetch(sems, (gate_weight, out.at[:256]), (up_weight, out.at[256:]))


def spread_kernel(packed, out):
    for t in range(16):
        out[t] = packed[...]


def came_from(base, i):
    return lax.rem(base - i + 8, 8)


def transpose_kernel(gu, out):
    out[:, :256] = gu[:256, :].T
    out[:, 256:] = gu[256:, :].T


def forward_kernel(
    rows, gu0, gu1, down0, down1, out, own_out, oth_out, wide, parts, x_own, x_oth, sems
):
    place = here()
    for far in range(2):
        for i in range(8):
            at = (far * 8 + i) * 88
            wide[at : at + 88, :] = rows[came_from(place[2], i) * 2 + lax.rem(far + place[4], 2)].astype(F32)
    blank = jnp.zeros((PADDED - QUARTER, 128), F32)
    for far in range(2):
        for j in range(8):
            piece = jnp.concatenate([wide[pl.ds(far * 704 + j, QUARTER, stride=8), :], blank], axis=0)
            at = (j // 4 * 2 + j % 2) * 128
            ref = (x_own, x_oth)[j % 4 // 2]
            ref[far * PADDED : (far + 1) * PADDED, at : at + 128] = piece.astype(BF16)
    by_cols = (((1,), (0,)), ((), ()))
    by_rows = (((1,), (1,)), ((), ()))
    copies = [
        pltpu.make_async_copy(x_own, own_out, sems.at[3]),
        pltpu.make_async_copy(x_oth, oth_out, sems.at[4]),
    ]
    for copy in copies:
        copy.start()
    for m in range(3):
        cols, dims = (slice(256, 512), by_rows) if m == 2 else (slice(0, 256), by_cols)
        own, oth = (down0[...], down1[...]) if m == 2 else (gu[m * 256 : (m + 1) * 256, :] for gu in (gu0, gu1))
        total = lax.dot_general(x_own[:, cols], own, dims, preferred_element_type=F32)
        total = total + lax.dot_general(x_oth[:, cols], oth, dims, preferred_element_type=F32)
        put_tiles(parts, m, total[:PADDED], place[1])
        put_tiles(parts, m, total[PADDED:], 1 - place[1])
        which = pl.ds(m * SIZE, SIZE)
        copies.append(pltpu.make_async_copy(parts.at[:, which], out.at[:, which], sems.at[m]))
        copies[-1].start()
    for copy in copies:
        copy.wait()


def activation_kernel(parts, acts):
    total = parts[0].astype(F32)
    for i in range(1, 16):
        total = total + parts[i].astype(F32)
    gate, up, back = total[:SIZE], total[SIZE : 2 * SIZE], total[2 * SIZE :]
    logistic = jax.nn.sigmoid(gate)
    hidden = (gate * logistic * up).astype(BF16)
    grad_gate_act = (back * up * logistic * (1.0 + gate * (1.0 - logistic))).astype(BF16)
    grad_up_act = (back * gate * logistic).astype(BF16)
    for i in range(8):
        acts[i, :SIZE, :] = grad_gate_act
        acts[i, SIZE : 2 * SIZE, :] = grad_up_act
        acts[i, 2 * SIZE :, :] = hidden


HALVES = (pl.ds(0, 448), pl.ds(448, 448))


def token_grad_kernel(acts, gu0, gu1, t2_hbm, t3_hbm, out, gate_act, up_act, wide, ts, sems):
    copies = [
        [pltpu.make_async_copy(t_hbm.at[rows], ts.at[k, rows], sems.at[k, i]) for i, rows in enumerate(parts)]
        for k, t_hbm, parts in ((0, t2_hbm, HALVES), (1, t3_hbm, HALVES))
    ]
    for copy in copies[0] + copies[1]:
        copy.start()
    get_tiles(acts, 0, gate_act, 0)
    get_tiles(acts, 1, up_act, 0)
    place = here()
    contract_cols = (((1,), (1,)), ((), ()))
    for k in range(4):
        if k < 2:
            gu = (gu0, gu1)[k]
            part = lax.dot_general(gate_act[...], gu[:256, :], contract_cols, preferred_element_type=F32)
            part = part + lax.dot_general(up_act[...], gu[256:, :], contract_cols, preferred_element_type=F32)
        else:
            for copy in copies[k - 2]:
                copy.wait()
            part = jnp.dot(gate_act[...], ts[k - 2, :, :256], preferred_element_type=F32)
            part = part + jnp.dot(up_act[...], ts[k - 2, :, 256:], preferred_element_type=F32)
        for j in range(2):
            wide[k // 2, pl.ds(k % 2 * 2 + j, QUARTER, stride=4), :] = tile(part[:QUARTER], j)
    wide[:, 4 * QUARTER :, :] = jnp.zeros((2, 8, 128), F32)
    for far in range(2):
        for i in range(8):
            rows = wide[far, i * 4 * ROWS : i * 4 * ROWS + BLOCK, :]
            out[came_from(place[2 + far], i) * 2 + lax.rem(far + place[4], 2)] = rows.astype(BF16)


def token_sum_kernel(parts, out, total):
    odd = here()[0] == 1
    acc = parts[0].astype(F32)
    for t in range(1, 16):
        acc = acc + parts[t].astype(F32)
    total[...] = acc
    pieces = [total[pl.ds(j, ROWS, stride=4), :] for j in range(4)]
    for j in range(4):
        out[:, j * 128 : (j + 1) * 128] = jnp.where(odd, pieces[(j + 2) % 4], pieces[j]).astype(BF16)


def weight_grad_kernel(x_own, x_got, acts0, acts1, acts2, acts3, grad_gate, grad_up, grad_down, x, act):
    contract_rows = (((0,), (0,)), ((), ()))
    for k in range(4):
        rows = slice(k // 2 * PADDED, (k // 2 + 1) * PADDED)
        x[k * PADDED : (k + 1) * PADDED, :] = (x_got if k % 2 else x_own)[rows, :]
    for m in range(3):
        for k, acts in enumerate((acts0, acts1, acts2, acts3)):
            get_tiles(acts, m, act, k * PADDED)
        if m < 2:
            out, left, right = (grad_gate, grad_up)[m], x[:, :256], act[...]
        else:
            out, left, right = grad_down, act[...], x[:, 256:]
        out[...] = lax.dot_general(left, right, contract_rows, preferred_element_type=F32).astype(BF16)


def copy_kernel(x, out):
    out[...] = x[...]


def after(x, *deps):
    return call(copy_kernel, (shape(*x.shape, dtype=x.dtype),), (x,), deps=deps, token=False)[0]


def after_in_hbm(x, *deps):
    return pl.pallas_call(
        lambda *refs: None,
        out_shape=pltpu.HBM(x.shape, x.dtype),
        in_specs=[HBM] + [VMEM] * len(deps),
        out_specs=HBM,
        input_output_aliases={0: 0},
        compiler_params=PARAMS,
    )(in_hbm(x), *deps)


def in_hbm(x):
    return pltpu.with_memory_space_constraint(x, pltpu.HBM)


def swap(axis, x):
    return lax.ppermute(x, axis, [(0, 1), (1, 0)])


def place_of(z, xh, core, xl, y):
    return (((z * 2 + xh) * 2 + core) * 2 + xl) * 8 + y


def permutation(to):
    grid = [(z, xh, c, xl, y) for z in range(8) for xh in range(2) for c in range(2) for xl in range(2) for y in range(8)]
    return [(place_of(*at), place_of(*to(*at))) for at in grid]


def per_device(tokens, cotangent, gate_weight, up_weight, down_weight):
    def chip(z, xl, y):
        return 4 * xl + y // 2, (y + 4 - z + 4 * xl + y // 2) % 8

    def forth(z, xh, c, xl, y):
        to, row = chip(z, xl, y)
        return to, y % 2, c, xh ^ y % 2 ^ xl, row

    def back(z, xh, c, xl, y):
        to, row = chip(z, xl, y)
        return to, xh, c, xh ^ y % 2 ^ xl, row

    there = permutation(forth)
    home = [(b, a) for a, b in permutation(back)]

    packed, ready0 = call(
        pack_kernel,
        (shape(88, 128),),
        (tokens, cotangent),
        [pltpu.VMEM((96, 128), F32)],
    )
    packed = lax.ppermute(packed, ALL, there)
    (spread,) = call(spread_kernel, (shape(16, 88, 128),), (packed,), flops=10**11, token=False)
    rows = lax.all_to_all(spread, AROUND, 0, 0, tiled=True)
    (gu0,) = call(
        weights_kernel,
        (shape(512, 896),),
        (in_hbm(gate_weight), in_hbm(up_weight)),
        [pltpu.SemaphoreType.DMA((2,))],
        specs=[HBM, HBM],
        deps=(ready0,),
        token=False,
    )
    gu1, down1 = swap("core", gu0), swap("core", down_weight)

    parts, x_own, x_oth, ready = call(
        forward_kernel,
        (pltpu.HBM((16, 3 * SIZE, 128), BF16), *[pltpu.HBM((2 * PADDED, 512), BF16)] * 2),
        (rows, gu0, gu1, down_weight, down1),
        [
            pltpu.VMEM((17 * 88, 128), F32),
            pltpu.VMEM((16, 3 * SIZE, 128), BF16),
            pltpu.VMEM((2 * PADDED, 512), BF16),
            pltpu.VMEM((2 * PADDED, 512), BF16),
            pltpu.SemaphoreType.DMA((5,)),
        ],
        outs=[HBM] * 3,
    )
    parts = lax.all_to_all(parts, ("xh", "z"), 0, 0, tiled=True)
    x_got = swap("core", after(x_oth, ready))
    (t0,) = call(transpose_kernel, (shape(896, 512),), (gu0,), deps=(ready,), token=False)
    t2 = swap("xh", t0)

    acts0, ready = call(activation_kernel, (shape(8, 3 * SIZE, 128),), (parts,))
    acts0 = lax.all_to_all(acts0, "z", 0, 0, tiled=True)
    t2 = after_in_hbm(t2, ready, x_got)
    t3 = swap("core", t2)
    (token_parts,) = call(
        token_grad_kernel,
        (shape(16, BLOCK, 128),),
        (acts0, gu0, gu1, in_hbm(t2), in_hbm(t3)),
        [
            pltpu.VMEM((PADDED, 896), BF16),
            pltpu.VMEM((PADDED, 896), BF16),
            pltpu.VMEM((2, 4 * QUARTER + 8, 128), F32),
            pltpu.VMEM((2, 896, 512), BF16),
            pltpu.SemaphoreType.DMA((2, 2)),
        ],
        specs=[VMEM] * 3 + [HBM] * 2,
        token=False,
    )
    token_parts = lax.all_to_all(token_parts, AROUND, 0, 0, tiled=True)
    acts2 = swap("xh", acts0)
    acts1 = swap("core", acts0)
    acts3 = swap("core", acts2)

    (grad_tokens,) = call(
        token_sum_kernel,
        (shape(ROWS, 512),),
        (token_parts,),
        [pltpu.VMEM((BLOCK, 128), F32)],
        flops=10**11,
        token=False,
    )
    grad_tokens = lax.ppermute(grad_tokens, ALL, home)

    grad_gate, grad_up, grad_down, ready = call(
        weight_grad_kernel,
        (shape(256, 896), shape(256, 896), shape(896, 256)),
        (x_own, x_got, acts0, acts1, acts2, acts3),
        [pltpu.VMEM((4 * PADDED, 512), BF16), pltpu.VMEM((4 * PADDED, 896), BF16)],
    )
    return (after(grad_tokens, ready), grad_gate, grad_up, grad_down)


def solution(mesh):
    chips = Mesh(mesh.devices.reshape(8, 2, 2, 2, 8), ALL)
    rows, cols = P(FSDP, TENSOR), P(TENSOR, FSDP)
    return jax.shard_map(
        per_device,
        mesh=chips,
        in_specs=(rows, rows, rows, rows, cols),
        out_specs=(rows, rows, rows, cols),
        check_vma=False,
    )
```

```python
import math

import jax
import jax.numpy as jnp
from jax import lax
from jax.experimental import pallas as pl
from jax.experimental.pallas import tpu as pltpu
from jax.sharding import Mesh
from jax.sharding import PartitionSpec as P

F32, BF16 = jnp.float32, jnp.bfloat16
ALL = ("z", "xh", "core", "xl", "y")
FSDP = ("z", "xh", "core")
TENSOR = ("xl", "y")
AROUND = ("y", "xl")

ROWS, QUARTER, PADDED = 11, 88, 96
BLOCK = 48
UP, ACROSS, PER = 5, 7, 5
SIZE = PER * 16
VMEM = pl.BlockSpec(memory_space=pltpu.VMEM)
HBM = pl.BlockSpec(memory_space=pltpu.HBM)
PARAMS = pltpu.CompilerParams(vmem_limit_bytes=20 * 1024 * 1024)


def call(kernel, out_shape, inputs, scratch=(), specs=None, flops=0, deps=(), outs=None, token=True):
    moved = sum(x.size * x.dtype.itemsize for x in inputs)
    moved += sum(math.prod(s.shape) * s.dtype.itemsize for s in out_shape)
    n, m = len(inputs), len(out_shape)

    def body(*refs):
        rest = refs[n + len(deps) :]
        if token:
            rest[m][...] = jnp.zeros((8, 128), F32)
        kernel(*refs[:n], *rest[:m], *rest[m + token :])

    return pl.pallas_call(
        body,
        out_shape=(*out_shape, *[shape(8, 128, dtype=F32)] * token),
        in_specs=list(specs or [VMEM] * n) + [VMEM] * len(deps),
        out_specs=list(outs or [VMEM] * m) + [VMEM] * token,
        scratch_shapes=list(scratch),
        compiler_params=PARAMS,
        cost_estimate=pl.CostEstimate(flops=flops, bytes_accessed=moved, transcendentals=0),
    )(*inputs, *deps)


def shape(*dims, dtype=BF16):
    return jax.ShapeDtypeStruct(dims, dtype)


def tile(ref_or_value, j):
    return ref_or_value[:, j * 128 : (j + 1) * 128]


def fetch(sems, *pairs):
    copies = [pltpu.make_async_copy(source, to, sems.at[i]) for i, (source, to) in enumerate(pairs)]
    for copy in copies:
        copy.start()
    for copy in copies:
        copy.wait()


def here():
    z, xh, core = (lax.axis_index(axis) for axis in FSDP)
    base = z + 4 + lax.rem(z, 4) * 2
    return core, xh, lax.rem(base + xh, 8), lax.rem(base + 1 - xh, 8), z // 4


def pack_kernel(both, out, wide):
    odd = here()[0] == 1
    for base in (0, 4):
        rows = both[:, base * 128 : (base + 4) * 128].astype(F32)
        for j in range(4):
            piece = jnp.where(odd, tile(rows, (j + 2) % 4), tile(rows, j))
            wide[pl.ds(base + j, ROWS, stride=8), :] = piece
    out[...] = wide[:88, :].astype(BF16)


def put_tiles(out, m, value, half):
    def put(slot, rows):
        row = m * SIZE + slot % PER * 16
        out[half * 8 + slot // PER, row : row + 16, :] = rows.astype(BF16)

    blank = jnp.zeros((8, 128), F32)
    for i in range(UP):
        for j in range(ACROSS):
            put(i * ACROSS + j, tile(value[i * 16 : (i + 1) * 16], j))
    last = [tile(value[UP * 16 : QUARTER], j) for j in range(ACROSS)] + [blank] * 3
    for j in range(0, 10, 2):
        put(UP * ACROSS + j // 2, jnp.concatenate([last[j], last[j + 1]], axis=0))


def get_tiles(ref, m, out, first):
    def get(slot):
        row = m * SIZE + slot % PER * 16
        return ref[slot // PER, row : row + 16, :]

    blank = jnp.zeros((8, 128), F32)
    for i in range(UP):
        for j in range(ACROSS):
            out[first + i * 16 : first + (i + 1) * 16, j * 128 : (j + 1) * 128] = get(i * ACROSS + j)
    for j in range(ACROSS):
        pair = get(UP * ACROSS + j // 2).astype(F32)
        half = pair[8:] if j % 2 else pair[:8]
        rows = jnp.concatenate([half, blank], axis=0).astype(BF16)
        out[first + UP * 16 : first + PADDED, j * 128 : (j + 1) * 128] = rows


def weights_kernel(gate_weight, up_weight, out, sems):
    fetch(sems, (gate_weight, out.at[:256]), (up_weight, out.at[256:]))


def spread_kernel(packed, out):
    for t in range(16):
        out[t] = packed[...]


def came_from(base, i):
    return lax.rem(base - i + 8, 8)


def transpose_kernel(gu, out):
    out[:, :256] = gu[:256, :].T
    out[:, 256:] = gu[256:, :].T


def forward_kernel(
    rows, gu0, gu1, down0, down1, out, own_out, oth_out, wide, parts, x_own, x_oth, sems
):
    place = here()
    for far in range(2):
        for i in range(8):
            at = (far * 8 + i) * 88
            wide[at : at + 88, :] = rows[came_from(place[2], i) * 2 + lax.rem(far + place[4], 2)].astype(F32)
    blank = jnp.zeros((PADDED - QUARTER, 128), F32)
    for far in range(2):
        for j in range(8):
            piece = jnp.concatenate([wide[pl.ds(far * 704 + j, QUARTER, stride=8), :], blank], axis=0)
            at = (j // 4 * 2 + j % 2) * 128
            ref = (x_own, x_oth)[j % 4 // 2]
            ref[far * PADDED : (far + 1) * PADDED, at : at + 128] = piece.astype(BF16)
    by_cols = (((1,), (0,)), ((), ()))
    by_rows = (((1,), (1,)), ((), ()))
    copies = [
        pltpu.make_async_copy(x_own, own_out, sems.at[3]),
        pltpu.make_async_copy(x_oth, oth_out, sems.at[4]),
    ]
    for copy in copies:
        copy.start()
    for m in range(3):
        cols, dims = (slice(256, 512), by_rows) if m == 2 else (slice(0, 256), by_cols)
        own, oth = (down0[...], down1[...]) if m == 2 else (gu[m * 256 : (m + 1) * 256, :] for gu in (gu0, gu1))
        total = lax.dot_general(x_own[:, cols], own, dims, preferred_element_type=F32)
        total = total + lax.dot_general(x_oth[:, cols], oth, dims, preferred_element_type=F32)
        put_tiles(parts, m, total[:PADDED], place[1])
        put_tiles(parts, m, total[PADDED:], 1 - place[1])
        which = pl.ds(m * SIZE, SIZE)
        copies.append(pltpu.make_async_copy(parts.at[:, which], out.at[:, which], sems.at[m]))
        copies[-1].start()
    for copy in copies:
        copy.wait()


def activation_kernel(parts, acts):
    total = parts[0].astype(F32)
    for i in range(1, 16):
        total = total + parts[i].astype(F32)
    gate, up, back = total[:SIZE], total[SIZE : 2 * SIZE], total[2 * SIZE :]
    logistic = jax.nn.sigmoid(gate)
    hidden = (gate * logistic * up).astype(BF16)
    grad_gate_act = (back * up * logistic * (1.0 + gate * (1.0 - logistic))).astype(BF16)
    grad_up_act = (back * gate * logistic).astype(BF16)
    for i in range(8):
        acts[i, :SIZE, :] = grad_gate_act
        acts[i, SIZE : 2 * SIZE, :] = grad_up_act
        acts[i, 2 * SIZE :, :] = hidden


HALVES = (pl.ds(0, 448), pl.ds(448, 448))


def token_grad_kernel(acts, gu0, gu1, t2_hbm, t3_hbm, out, gate_act, up_act, wide, ts, sems):
    copies = [
        [pltpu.make_async_copy(t_hbm.at[rows], ts.at[k, rows], sems.at[k, i]) for i, rows in enumerate(parts)]
        for k, t_hbm, parts in ((0, t2_hbm, HALVES), (1, t3_hbm, HALVES))
    ]
    for copy in copies[0] + copies[1]:
        copy.start()
    get_tiles(acts, 0, gate_act, 0)
    get_tiles(acts, 1, up_act, 0)
    place = here()
    contract_cols = (((1,), (1,)), ((), ()))
    for k in range(4):
        if k < 2:
            gu = (gu0, gu1)[k]
            part = lax.dot_general(gate_act[...], gu[:256, :], contract_cols, preferred_element_type=F32)
            part = part + lax.dot_general(up_act[...], gu[256:, :], contract_cols, preferred_element_type=F32)
        else:
            for copy in copies[k - 2]:
                copy.wait()
            part = jnp.dot(gate_act[...], ts[k - 2, :, :256], preferred_element_type=F32)
            part = part + jnp.dot(up_act[...], ts[k - 2, :, 256:], preferred_element_type=F32)
        for j in range(2):
            wide[k // 2, pl.ds(k % 2 * 2 + j, QUARTER, stride=4), :] = tile(part[:QUARTER], j)
    wide[:, 4 * QUARTER :, :] = jnp.zeros((2, 8, 128), F32)
    for far in range(2):
        for i in range(8):
            rows = wide[far, i * 4 * ROWS : i * 4 * ROWS + BLOCK, :]
            out[came_from(place[2 + far], i) * 2 + lax.rem(far + place[4], 2)] = rows.astype(BF16)


def token_sum_kernel(parts, out, total):
    odd = here()[0] == 1
    acc = parts[0].astype(F32)
    for t in range(1, 16):
        acc = acc + parts[t].astype(F32)
    total[...] = acc
    pieces = [total[pl.ds(j, ROWS, stride=4), :] for j in range(4)]
    for j in range(4):
        out[:, j * 128 : (j + 1) * 128] = jnp.where(odd, pieces[(j + 2) % 4], pieces[j]).astype(BF16)


def weight_grad_kernel(x_own, x_got, acts0, acts1, acts2, acts3, grad_gate, grad_up, grad_down, x, act):
    contract_rows = (((0,), (0,)), ((), ()))
    for k in range(4):
        rows = slice(k // 2 * PADDED, (k // 2 + 1) * PADDED)
        x[k * PADDED : (k + 1) * PADDED, :] = (x_got if k % 2 else x_own)[rows, :]
    for m in range(3):
        for k, acts in enumerate((acts0, acts1, acts2, acts3)):
            get_tiles(acts, m, act, k * PADDED)
        if m < 2:
            out, left, right = (grad_gate, grad_up)[m], x[:, :256], act[...]
        else:
            out, left, right = grad_down, act[...], x[:, 256:]
        out[...] = lax.dot_general(left, right, contract_rows, preferred_element_type=F32).astype(BF16)


def copy_kernel(x, out):
    out[...] = x[...]


def after(x, *deps):
    return call(copy_kernel, (shape(*x.shape, dtype=x.dtype),), (x,), deps=deps, token=False)[0]


def after_in_hbm(x, *deps):
    return pl.pallas_call(
        lambda *refs: None,
        out_shape=pltpu.HBM(x.shape, x.dtype),
        in_specs=[HBM] + [VMEM] * len(deps),
        out_specs=HBM,
        input_output_aliases={0: 0},
        compiler_params=PARAMS,
    )(in_hbm(x), *deps)


def in_hbm(x):
    return pltpu.with_memory_space_constraint(x, pltpu.HBM)


def swap(axis, x):
    return lax.ppermute(x, axis, [(0, 1), (1, 0)])


def place_of(z, xh, core, xl, y):
    return (((z * 2 + xh) * 2 + core) * 2 + xl) * 8 + y


def permutation(to):
    grid = [(z, xh, c, xl, y) for z in range(8) for xh in range(2) for c in range(2) for xl in range(2) for y in range(8)]
    return [(place_of(*at), place_of(*to(*at))) for at in grid]


def per_device(tokens, cotangent, gate_weight, up_weight, down_weight):
    def chip(z, xl, y):
        return 4 * xl + y // 2, (y + 4 - z + 4 * xl + y // 2) % 8

    def forth(z, xh, c, xl, y):
        to, row = chip(z, xl, y)
        return to, y % 2, c, xh ^ y % 2 ^ xl, row

    def back(z, xh, c, xl, y):
        to, row = chip(z, xl, y)
        return to, xh, c, xh ^ y % 2 ^ xl, row

    there = permutation(forth)
    home = [(b, a) for a, b in permutation(back)]

    packed, ready0 = call(
        pack_kernel,
        (shape(88, 128),),
        (jnp.concatenate([tokens, cotangent], axis=1),),
        [pltpu.VMEM((96, 128), F32)],
    )
    packed = lax.ppermute(packed, ALL, there)
    (spread,) = call(spread_kernel, (shape(16, 88, 128),), (packed,), flops=10**11, token=False)
    rows = lax.all_to_all(spread, AROUND, 0, 0, tiled=True)
    (gu0,) = call(
        weights_kernel,
        (shape(512, 896),),
        (in_hbm(gate_weight), in_hbm(up_weight)),
        [pltpu.SemaphoreType.DMA((2,))],
        specs=[HBM, HBM],
        deps=(ready0,),
        token=False,
    )
    gu1, down1 = swap("core", gu0), swap("core", down_weight)

    parts, x_own, x_oth, ready = call(
        forward_kernel,
        (pltpu.HBM((16, 3 * SIZE, 128), BF16), *[pltpu.HBM((2 * PADDED, 512), BF16)] * 2),
        (rows, gu0, gu1, down_weight, down1),
        [
            pltpu.VMEM((17 * 88, 128), F32),
            pltpu.VMEM((16, 3 * SIZE, 128), BF16),
            pltpu.VMEM((2 * PADDED, 512), BF16),
            pltpu.VMEM((2 * PADDED, 512), BF16),
            pltpu.SemaphoreType.DMA((5,)),
        ],
        outs=[HBM] * 3,
    )
    parts = lax.all_to_all(parts, ("xh", "z"), 0, 0, tiled=True)
    x_got = swap("core", after(x_oth, ready))
    (t0,) = call(transpose_kernel, (shape(896, 512),), (gu0,), deps=(ready,), token=False)
    t2 = swap("xh", t0)

    acts0, ready = call(activation_kernel, (shape(8, 3 * SIZE, 128),), (parts,))
    acts0 = lax.all_to_all(acts0, "z", 0, 0, tiled=True)
    t2 = after_in_hbm(t2, ready, x_got)
    t3 = swap("core", t2)
    (token_parts,) = call(
        token_grad_kernel,
        (shape(16, BLOCK, 128),),
        (acts0, gu0, gu1, in_hbm(t2), in_hbm(t3)),
        [
            pltpu.VMEM((PADDED, 896), BF16),
            pltpu.VMEM((PADDED, 896), BF16),
            pltpu.VMEM((2, 4 * QUARTER + 8, 128), F32),
            pltpu.VMEM((2, 896, 512), BF16),
            pltpu.SemaphoreType.DMA((2, 2)),
        ],
        specs=[VMEM] * 3 + [HBM] * 2,
        token=False,
    )
    token_parts = lax.all_to_all(token_parts, AROUND, 0, 0, tiled=True)
    acts2 = swap("xh", acts0)
    acts1 = swap("core", acts0)
    acts3 = swap("core", acts2)

    (grad_tokens,) = call(
        token_sum_kernel,
        (shape(ROWS, 512),),
        (token_parts,),
        [pltpu.VMEM((BLOCK, 128), F32)],
        flops=10**11,
        token=False,
    )
    grad_tokens = lax.ppermute(grad_tokens, ALL, home)

    grad_gate, grad_up, grad_down, ready = call(
        weight_grad_kernel,
        (shape(256, 896), shape(256, 896), shape(896, 256)),
        (x_own, x_got, acts0, acts1, acts2, acts3),
        [pltpu.VMEM((4 * PADDED, 512), BF16), pltpu.VMEM((4 * PADDED, 896), BF16)],
    )
    return (after(grad_tokens, ready), grad_gate, grad_up, grad_down)


def solution(mesh):
    chips = Mesh(mesh.devices.reshape(8, 2, 2, 2, 8), ALL)
    rows, cols = P(FSDP, TENSOR), P(TENSOR, FSDP)
    return jax.shard_map(
        per_device,
        mesh=chips,
        in_specs=(rows, rows, rows, rows, cols),
        out_specs=(rows, rows, rows, cols),
        check_vma=False,
    )
```
